32 devices in a mesh: cand: 4 (over x, core), seq: 8 (over z, y).
Axes of the slice: x: 2, y: 2, z: 4, core: 2. Of those that a mesh axis runs over, the one named last changes fastest.
Arguments:
- hyena_query: bfloat16 [4, 1024, 4096], P('cand', 'seq'), may hold values from -6 to 6
- hyena_key: bfloat16 [4, 1024, 4096], P('cand', 'seq'), may hold values from -6 to 6
- hyena_value: bfloat16 [4, 1024, 4096], P('cand', 'seq'), may hold values from -6 to 6
- hyena_filters: float32 [128, 256], replicated, may hold values from -0.5 to 0.5
- context_tail: bfloat16 [127, 4096], replicated, may hold values from -6 to 6
- cont_queries: bfloat16 [4, 1024, 32, 128], P('cand', 'seq'), may hold values from -100 to 100
- cont_keys: bfloat16 [4, 1024, 32, 128], P('cand', 'seq'), may hold values from -5 to 5
- cont_values: bfloat16 [4, 1024, 32, 128], P('cand', 'seq'), may hold values from -6 to 6
- context_keys: bfloat16 [768, 32, 128], P('seq'), may hold values from -6 to 6
- context_values: bfloat16 [768, 32, 128], P('seq'), may hold values from -6 to 6
- lengths: int32 [4], P('cand'), may hold values from 256 to 1024, as said below
Outputs:
- hyena_out: bfloat16 [4, 1024, 4096], P('cand', 'seq')
- attention_out: bfloat16 [4, 1024, 32, 128], P('cand', 'seq')
The draws below stay inside these ranges and needn't reach their ends.
Inputs may be any that keep to these rules, and one draw needn't show every extreme that they name: `lengths`: positions of a candidate at or past its length are padding; some candidate has all 1024 positions valid.
All inputs are finite; a program needn't handle non-finite values.
Results may differ from the reference program's by a relative error of at most 0.0049.
Values may be sent and summed in bfloat16 or wider, within the bound.
No kernel may reach another device: no remote copies, remote signals or barrier semaphores. Data moves between devices by JAX's collectives and lax.ppermute only.
A program may use at most 64 MiB of HBM per device.

```python
import math
import jax
import jax.numpy as jnp
from jax import lax

CH = 4096
CH_GROUP = 16
FILT = 128
HEADS = 32
HD = 128
CAND = 4
LEN = 1024
CTX = 768
FGROUPS = 256


def paired_draws(key):
    base = jax.random.fold_in(key, 11)
    key_query, key_key = jax.random.split(base, 2)
    shape = (CAND, LEN, HEADS, HD)
    queries = jnp.clip(2.5 * jax.random.normal(key_query, shape, jnp.float32), -12.0, 12.0)
    key_rows = jnp.clip(jax.random.normal(key_key, shape, jnp.float32), -5.0, 5.0)
    return (queries, key_rows)


def draw_cont_queries(key, part):
    return paired_draws(key)[0].astype(jnp.bfloat16)


def draw_cont_keys(key, part):
    return paired_draws(key)[1].astype(jnp.bfloat16)


def draw_lengths(key, part):
    key_first, key_second = jax.random.split(jax.random.fold_in(key, 5))
    drawn = jax.random.randint(key_first, (CAND,), LEN // 4, LEN + 1)
    chosen = jax.random.randint(key_second, (), 0, CAND)
    return jnp.where(jnp.arange(CAND) == chosen, LEN, drawn).astype(jnp.int32)


def block_levels(own_key, extent, cuts, low, top_value):
    def one(dim, shards_of):
        steps = jax.random.uniform(jax.random.fold_in(jax.random.fold_in(own_key, 6), dim), (shards_of,), jnp.float32, low / len(cuts), top_value / len(cuts))
        return jnp.repeat(jnp.exp(steps), extent[dim] // shards_of).reshape((-1,) + (1,) * (len(extent) - dim - 1))

    gain = one(*cuts[0])
    for cut in cuts[1:]:
        gain = gain * one(*cut)
    return gain


def scatter_about(own_key, extent, scale, most, shards=(), held_as=jnp.bfloat16):
    values = jax.random.normal(own_key, extent, jnp.float32) * scale
    if len(shards) > 0:
        values = block_levels(own_key, extent, shards, -0.22, 0.18) * values
    return jnp.clip(values, min=-most, max=most).astype(held_as)


def setup_inputs(seed: int = 0) -> dict:
    key_of = jax.random.split(jax.random.key(seed), 12)
    return {
        "hyena_query": scatter_about(key_of[0], (CAND, LEN, CH), 1.0, 6.0, ((0, 4), (1, 8))),
        "hyena_key": scatter_about(key_of[1], (CAND, LEN, CH), 1.0, 6.0, ((0, 4), (1, 8))),
        "hyena_value": scatter_about(key_of[2], (CAND, LEN, CH), 1.0, 6.0, ((0, 4), (1, 8))),
        "hyena_filters": scatter_about(key_of[3], (FILT, FGROUPS), FILT ** -0.5, 0.5, (), jnp.float32),
        "context_tail": scatter_about(key_of[4], (FILT - 1, CH), 1.0, 6.0),
        "cont_queries": draw_cont_queries(jax.random.fold_in(key_of[11], 71), 0),
        "cont_keys": draw_cont_keys(jax.random.fold_in(key_of[11], 71), 0),
        "cont_values": scatter_about(key_of[7], (CAND, LEN, HEADS, HD), 1.0, 6.0, ((0, 4), (1, 8))),
        "context_keys": scatter_about(key_of[8], (CTX, HEADS, HD), 1.0, 6.0, ((0, 8),)),
        "context_values": scatter_about(key_of[9], (CTX, HEADS, HD), 1.0, 6.0, ((0, 8),)),
        "lengths": draw_lengths(jax.random.fold_in(key_of[11], 71), 0),
    }


masked_score = -1e+30

def reference(hyena_query, hyena_key, hyena_value, hyena_filters, context_tail, cont_queries, cont_keys, cont_values, context_keys, context_values, lengths):
    per_channel = jnp.repeat(hyena_filters, CH_GROUP, axis=1)
    places = jnp.arange(LEN)

    def hyena_one(operands):
        query_rows, key_rows, value_rows, length_one = operands
        product = (key_rows.astype(jnp.float32) * value_rows.astype(jnp.float32)).astype(jnp.bfloat16)
        extended = jnp.concatenate([context_tail, product], axis=0).astype(jnp.float32)

        def add_tap(offset, running):
            start = (FILT - 1 - offset).astype(jnp.int32)
            return running + per_channel[offset][None, :] * lax.dynamic_slice_in_dim(extended, start, LEN, 0)
        convolved = lax.fori_loop(0, FILT, add_tap, jnp.zeros((LEN, CH), jnp.float32))
        keep = places < length_one
        return jnp.where(keep[:, None], query_rows.astype(jnp.float32) * convolved, 0.0).astype(jnp.bfloat16)
    hyena_out = lax.map(hyena_one, (hyena_query, hyena_key, hyena_value, lengths))
    block_rows = min(512, LEN)
    count = LEN // block_rows
    scaling = 1.0 / math.sqrt(HD)

    def head_one(operands):
        query_rows, key_rows, value_rows, context_key_rows, context_value_rows = operands
        all_keys = jnp.concatenate([context_key_rows, key_rows], axis=0)
        all_values = jnp.concatenate([context_value_rows, value_rows], axis=0)

        def block_one(index):
            start = (index * block_rows).astype(jnp.int32)
            query_block = lax.dynamic_slice_in_dim(query_rows, start, block_rows, 0)
            scores = jnp.dot(query_block, all_keys.T, preferred_element_type=jnp.float32) * scaling
            query_places = index * block_rows + jnp.arange(block_rows)
            allowed = jnp.concatenate([jnp.ones((block_rows, CTX), jnp.bool_), places[None, :] <= query_places[:, None]], axis=1)
            scores = jnp.where(allowed, scores, masked_score)
            highest = lax.optimization_barrier(jnp.max(scores, axis=1, keepdims=True))
            weights = jnp.exp(scores - highest)
            totals = lax.optimization_barrier(jnp.sum(weights, axis=1))
            mixed = jnp.dot(weights.astype(jnp.bfloat16), all_values, preferred_element_type=jnp.float32)
            return mixed / totals[:, None]
        return lax.map(block_one, jnp.arange(count)).reshape(LEN, HD)

    def cand_one(operands):
        query_rows, key_rows, value_rows, length_one = operands
        result = lax.map(head_one, (query_rows.transpose(1, 0, 2), key_rows.transpose(1, 0, 2), value_rows.transpose(1, 0, 2), context_keys.transpose(1, 0, 2), context_values.transpose(1, 0, 2)))
        result = result.transpose(1, 0, 2)
        keep = places < length_one
        return jnp.where(keep[:, None, None], result, 0.0).astype(jnp.bfloat16)
    attention_out = lax.map(cand_one, (cont_queries, cont_keys, cont_values, lengths))
    return (hyena_out, attention_out)
```

```python
import functools
import math

import jax
import jax.numpy as jnp
from jax import lax
from jax.experimental import pallas as pl
from jax.experimental.pallas import tpu as pltpu
from jax.sharding import PartitionSpec as P

CH_GROUP = 16
LANES = 128

masked_score = -1e30


def hyena_kernel(length_ref, first_ref, query_ref, key_ref, value_ref, before_ref, tail_ref, wave_ref, out_ref):
    rows, lanes = key_ref.shape[1], key_ref.shape[2]
    product = (key_ref[0].astype(jnp.float32) * value_ref[0].astype(jnp.float32)).astype(jnp.bfloat16)
    first = jnp.broadcast_to(first_ref[0], (rows, lanes)) == 1
    earlier = jnp.where(first, tail_ref[...].astype(jnp.float32), before_ref[0].astype(jnp.float32))
    extended = jnp.concatenate([earlier.astype(jnp.bfloat16), product], axis=0)
    channel = lax.broadcasted_iota(jnp.int32, (rows, lanes), 1) // CH_GROUP
    convolved = jnp.zeros((rows, lanes), jnp.float32)
    for group in range(lanes // CH_GROUP):
        wave = jnp.broadcast_to(wave_ref[group : group + 1, :], (rows, 2 * rows))
        taps = pltpu.roll(wave, 0, 1, stride=1, stride_axis=0)
        high = taps.astype(jnp.bfloat16)
        low = (taps - high.astype(jnp.float32)).astype(jnp.bfloat16)
        term = jnp.dot(high, extended, preferred_element_type=jnp.float32) + jnp.dot(
            low, extended, preferred_element_type=jnp.float32
        )
        convolved = jnp.where(channel == group, term, convolved)
    places = lax.broadcasted_iota(jnp.int32, (rows, lanes), 0)
    gated = query_ref[0].astype(jnp.float32) * convolved
    out_ref[0] = jnp.where(places < length_ref[0], gated, 0.0).astype(jnp.bfloat16)


def hyena(query, key, value, received, tail, filters, left, first):
    _, rows, channels = key.shape
    wave = jnp.pad(filters[::-1], ((1, 2 * rows - filters.shape[0] - 1), (0, 0))).T
    tail = jnp.pad(tail, ((1, 0), (0, 0)))
    groups = LANES // CH_GROUP
    block = pl.BlockSpec((1, rows, LANES), lambda i: (0, 0, i))
    scalar = pl.BlockSpec(memory_space=pltpu.SMEM)
    return pl.pallas_call(
        hyena_kernel,
        grid=(channels // LANES,),
        out_shape=jax.ShapeDtypeStruct(query.shape, jnp.bfloat16),
        in_specs=[
            scalar,
            scalar,
            block,
            block,
            block,
            block,
            pl.BlockSpec((rows, LANES), lambda i: (0, i)),
            pl.BlockSpec((groups, 2 * rows), lambda i: (i, 0)),
        ],
        out_specs=block,
        cost_estimate=pl.CostEstimate(
            flops=2 * 2 * rows * 2 * rows * channels * groups, bytes_accessed=12 * rows * channels, transcendentals=0
        ),
        name="hyena",
    )(left, first, query, key, value, received, tail, wave)


def attend_kernel(block_rows, q_ref, k_ref, v_ref, ck_ref, cv_ref, out_ref):
    sources, _, rows, width = q_ref.shape
    length = sources * rows
    scaling = 1.0 / math.sqrt(width)
    context = ck_ref.shape[1] * ck_ref.shape[3]
    context_keys = ck_ref[0, :, 0].reshape(context, width)
    context_values = cv_ref[0, :, 0].reshape(context, width)
    per = block_rows // rows
    contract = (((1,), (1,)), ((), ()))
    for index in range(length // block_rows):
        queries = q_ref[index * per : (index + 1) * per, 0].reshape(block_rows, width)
        pieces = [
            (lax.dot_general(queries, context_keys, contract, preferred_element_type=jnp.float32), context_values)
        ]
        if index > 0:
            keys = k_ref[: index * per, 0].reshape(index * block_rows, width)
            values = v_ref[: index * per, 0].reshape(index * block_rows, width)
            pieces.append((lax.dot_general(queries, keys, contract, preferred_element_type=jnp.float32), values))
        keys = k_ref[index * per : (index + 1) * per, 0].reshape(block_rows, width)
        values = v_ref[index * per : (index + 1) * per, 0].reshape(block_rows, width)
        scores = lax.dot_general(queries, keys, contract, preferred_element_type=jnp.float32)
        shape = (block_rows, block_rows)
        allowed = lax.broadcasted_iota(jnp.int32, shape, 1) <= lax.broadcasted_iota(jnp.int32, shape, 0)
        pieces.append((jnp.where(allowed, scores, masked_score), values))
        highest = functools.reduce(jnp.maximum, [jnp.max(s, axis=1, keepdims=True) for s, _ in pieces])
        total = jnp.zeros((block_rows, 1), jnp.float32)
        mixed = jnp.zeros((block_rows, width), jnp.float32)
        for scores, values in pieces:
            weights = jnp.exp((scores - highest) * scaling)
            total += jnp.sum(weights, axis=1, keepdims=True)
            mixed += jnp.dot(weights.astype(jnp.bfloat16), values, preferred_element_type=jnp.float32)
        result = (mixed / total).astype(jnp.bfloat16)
        out_ref[index * per : (index + 1) * per, 0] = result.reshape(per, rows, width)


def attend(queries, keys, values, context):
    sources, heads, rows, width = queries.shape
    block_rows = rows * (2 if sources % 2 == 0 and sources * rows <= 2048 else 1)
    own = pl.BlockSpec((sources, 1, rows, width), lambda h: (0, h, 0, 0))

    def shared(which):
        return pl.BlockSpec((1, context.shape[1], 1) + context.shape[3:], lambda h: (h, 0, which, 0, 0))

    length, context_rows = sources * rows, context.shape[1] * context.shape[3]
    pairs = heads * length * (context_rows + (length + block_rows) // 2)
    return pl.pallas_call(
        functools.partial(attend_kernel, block_rows),
        grid=(heads,),
        out_shape=jax.ShapeDtypeStruct(queries.shape, jnp.bfloat16),
        in_specs=[own, own, own, shared(0), shared(1)],
        out_specs=own,
        cost_estimate=pl.CostEstimate(
            flops=4 * pairs * width, bytes_accessed=heads * width * (8 * length + 4 * context_rows), transcendentals=pairs
        ),
        compiler_params=pltpu.CompilerParams(vmem_limit_bytes=48 * 1024 * 1024),
        name="attend",
    )(queries, keys, values, context, context)


def local(
    hyena_query,
    hyena_key,
    hyena_value,
    hyena_filters,
    context_tail,
    cont_queries,
    cont_keys,
    cont_values,
    context_keys,
    context_values,
    lengths,
):
    peers = lax.axis_size("seq")
    cands = lax.axis_size("cand")
    me = lax.axis_index("seq")
    rows = hyena_key.shape[1]
    heads, width = cont_queries.shape[2:]
    share = heads // peers

    def by_owner(x):
        return x.reshape(x.shape[0], peers, share, width).transpose(1, 2, 0, 3)

    def exchange(x):
        return lax.all_to_all(x, "seq", split_axis=0, concat_axis=0, tiled=True)

    if share % cands == 0:
        part = share // cands
        mine = lax.axis_index("cand")

        def picked(x):
            cut = x.reshape(x.shape[0], peers, cands, part, width)
            return lax.dynamic_index_in_dim(cut, mine, 2, keepdims=False).transpose(1, 2, 0, 3)

        pair = jnp.stack([picked(context_keys), picked(context_values)], axis=2)
        pair = exchange(pair)
        context = lax.all_gather(pair.transpose(1, 0, 2, 3, 4), "cand", axis=0, tiled=True)
    else:
        pair = exchange(jnp.stack([by_owner(context_keys), by_owner(context_values)], axis=2))
        context = pair.transpose(1, 0, 2, 3, 4)

    queries = exchange(by_owner(cont_queries[0]))
    keys = exchange(by_owner(cont_keys[0]))
    values = exchange(by_owner(cont_values[0]))

    product = (hyena_key.astype(jnp.float32) * hyena_value.astype(jnp.float32)).astype(jnp.bfloat16)
    received = lax.ppermute(product, "seq", [(i, i + 1) for i in range(peers - 1)])
    left = lengths - me * rows
    first = (me == 0).astype(jnp.int32)[None]
    hyena_out = hyena(hyena_query, hyena_key, hyena_value, received, context_tail, hyena_filters, left, first)

    attended = exchange(attend(queries, keys, values, context))
    attention = attended.transpose(2, 0, 1, 3).reshape(1, rows, heads, width)
    keep = jnp.arange(rows)[None, :, None, None] < left[:, None, None, None]
    attention_out = jnp.where(keep, attention, jnp.zeros((), jnp.bfloat16))
    return (hyena_out, attention_out)


def solution(mesh):
    placed = (
        P("cand", "seq", None),
        P("cand", "seq", None),
        P("cand", "seq", None),
        P(),
        P(),
        P("cand", "seq", None, None),
        P("cand", "seq", None, None),
        P("cand", "seq", None, None),
        P("seq", None, None),
        P("seq", None, None),
        P("cand"),
    )
    return jax.shard_map(
        local,
        mesh=mesh,
        in_specs=placed,
        out_specs=(P("cand", "seq", None), P("cand", "seq", None, None)),
        check_vma=False,
    )
```

```python
import functools
import math

import jax
import jax.numpy as jnp
from jax import lax
from jax.experimental import pallas as pl
from jax.experimental.pallas import tpu as pltpu
from jax.sharding import PartitionSpec as P

CH_GROUP = 16
LANES = 128
VMEM = 56 * 1024 * 1024
WAVES = 2

masked_score = -1e30

bf16 = jnp.bfloat16
f32 = jnp.float32


def hyena_kernel(place_ref, query_ref, key_ref, value_ref, before_ref, tail_ref, wave_ref, out_ref):
    rows, lanes = key_ref.shape[1], key_ref.shape[2]
    product = (key_ref[0].astype(f32) * value_ref[0].astype(f32)).astype(bf16)
    first = jnp.broadcast_to(place_ref[0], (rows, lanes)) == 0
    earlier = jnp.where(first, tail_ref[...].astype(f32), before_ref[...].astype(f32))
    extended = jnp.concatenate([earlier.astype(bf16), product], axis=0)
    channel = lax.broadcasted_iota(jnp.int32, (rows, lanes), 1) // CH_GROUP
    convolved = jnp.zeros((rows, lanes), f32)
    for group in range(lanes // CH_GROUP):
        wave = jnp.broadcast_to(wave_ref[group : group + 1, :], (rows, 2 * rows))
        taps = pltpu.roll(wave, 0, 1, stride=1, stride_axis=0)
        high = taps.astype(bf16)
        low = (taps - high.astype(f32)).astype(bf16)
        term = jnp.dot(high, extended, preferred_element_type=f32) + jnp.dot(
            low, extended, preferred_element_type=f32
        )
        convolved = jnp.where(channel == group, term, convolved)
    places = lax.broadcasted_iota(jnp.int32, (rows, lanes), 0)
    gated = query_ref[0].astype(f32) * convolved
    out_ref[0] = jnp.where(places < place_ref[1], gated, 0.0).astype(bf16)


def hyena(query, key, value, received, tail, filters, place):
    _, rows, channels = key.shape
    wave = jnp.pad(filters[::-1], ((1, 2 * rows - filters.shape[0] - 1), (0, 0))).T
    tail = jnp.pad(tail, ((1, 0), (0, 0)))
    groups = LANES // CH_GROUP
    block = pl.BlockSpec((1, rows, LANES), lambda i: (0, 0, i))
    flat = pl.BlockSpec((rows, LANES), lambda i: (0, i))
    return pl.pallas_call(
        hyena_kernel,
        grid=(channels // LANES,),
        out_shape=jax.ShapeDtypeStruct(query.shape, bf16),
        in_specs=[
            pl.BlockSpec(memory_space=pltpu.SMEM),
            block,
            block,
            block,
            flat,
            flat,
            pl.BlockSpec((groups, 2 * rows), lambda i: (i, 0)),
        ],
        out_specs=block,
        cost_estimate=pl.CostEstimate(
            flops=2 * 2 * rows * 2 * rows * channels * groups, bytes_accessed=12 * rows * channels, transcendentals=0
        ),
        name="hyena",
    )(place, query, key, value, received, tail, wave)


def attend_kernel(block_rows, q_ref, k_ref, v_ref, ck_ref, cv_ref, out_ref):
    sources, _, rows, width = k_ref.shape
    index = pl.program_id(1)
    scaling = 1.0 / math.sqrt(width)
    context = ck_ref.shape[1] * ck_ref.shape[3]
    contract = (((1,), (1,)), ((), ()))
    queries = q_ref[...].reshape(block_rows, width)
    per = block_rows // rows

    def fold(carried, scores, values):
        run_max, run_total, mixed = carried
        highest = jnp.maximum(run_max, jnp.max(scores, axis=1, keepdims=True))
        weights = jnp.exp((scores - highest) * scaling)
        shrink = jnp.exp((run_max - highest) * scaling)
        total = run_total * shrink + jnp.sum(weights, axis=1, keepdims=True)
        mixed = mixed * shrink + jnp.dot(weights.astype(bf16), values, preferred_element_type=f32)
        return highest, total, mixed

    def own(block):
        keys = k_ref[pl.ds(block * per, per), 0].reshape(block_rows, width)
        values = v_ref[pl.ds(block * per, per), 0].reshape(block_rows, width)
        return lax.dot_general(queries, keys, contract, preferred_element_type=f32), values

    scores, values = own(index)
    shape = (block_rows, block_rows)
    allowed = lax.broadcasted_iota(jnp.int32, shape, 1) <= lax.broadcasted_iota(jnp.int32, shape, 0)
    scores = jnp.where(allowed, scores, masked_score)
    start = (
        jnp.full((block_rows, 1), masked_score, f32),
        jnp.zeros((block_rows, 1), f32),
        jnp.zeros((block_rows, width), f32),
    )
    carried = fold(start, scores, values)
    carried = lax.fori_loop(0, index, lambda i, c: fold(c, *own(i)), carried)
    context_keys = ck_ref[0, :, 0].reshape(context, width)
    context_values = cv_ref[0, :, 0].reshape(context, width)
    scores = lax.dot_general(queries, context_keys, contract, preferred_element_type=f32)
    _, total, mixed = fold(carried, scores, context_values)
    out_ref[...] = (mixed / total).astype(bf16).reshape(out_ref.shape)


def attend(queries, keys, values, context):
    sources, heads, rows, width = queries.shape
    per = 2 if sources % 2 == 0 else 1
    whole = pl.BlockSpec((sources, 1, rows, width), lambda h, i: (0, h, 0, 0))
    part = pl.BlockSpec((per, 1, rows, width), lambda h, i: (i, h, 0, 0))

    def shared(which):
        return pl.BlockSpec((1, context.shape[1], 1) + context.shape[3:], lambda h, i: (h, 0, which, 0, 0))

    length, context_rows = sources * rows, context.shape[1] * context.shape[3]
    pairs = heads * length * (context_rows + (length + rows * per) // 2)
    return pl.pallas_call(
        functools.partial(attend_kernel, rows * per),
        grid=(heads, sources // per),
        out_shape=jax.ShapeDtypeStruct(queries.shape, bf16),
        in_specs=[part, whole, whole, shared(0), shared(1)],
        out_specs=part,
        cost_estimate=pl.CostEstimate(
            flops=4 * pairs * width, bytes_accessed=heads * width * (8 * length + 4 * context_rows), transcendentals=pairs
        ),
        compiler_params=pltpu.CompilerParams(vmem_limit_bytes=VMEM),
        name="attend",
    )(queries, keys, values, context, context)


def attention_by_heads(cont_queries, cont_keys, cont_values, context_keys, context_values, left):
    peers = lax.axis_size("seq")
    rows, heads, width = cont_queries.shape
    share = heads // peers

    def by_owner(x):
        return x.reshape(x.shape[0], peers, share, width).transpose(1, 2, 0, 3)

    def exchange(x):
        return lax.all_to_all(x, "seq", split_axis=0, concat_axis=0, tiled=True)

    pair = exchange(jnp.stack([by_owner(context_keys), by_owner(context_values)], axis=2))
    context = pair.transpose(1, 0, 2, 3, 4)
    queries = exchange(by_owner(cont_queries))
    keys = exchange(by_owner(cont_keys))
    values = exchange(by_owner(cont_values))
    attended = exchange(attend(queries, keys, values, context))
    attention = attended.transpose(2, 0, 1, 3).reshape(rows, heads, width)
    keep = jnp.arange(rows)[:, None, None] < left
    return jnp.where(keep, attention, jnp.zeros((), bf16))


SIDE = 4


def pack_kernel(*refs):
    count = 3 * SIDE
    sources, outs = refs[1 : 1 + count], refs[1 + count :]
    group = sources[0].shape[1]
    each = group // WAVES
    for partner in range(SIDE):
        for which in range(3):
            x = jnp.transpose(sources[3 * partner + which][...].astype(f32), (1, 0, 2)).astype(bf16)
            outs[partner][which * group : (which + 1) * group] = x
            if which == 0:
                for wave in range(WAVES):
                    outs[SIDE + wave * SIDE + partner][...] = x[wave * each : (wave + 1) * each]


def pack(queries, keys, values, side):
    rows, heads, width = queries.shape
    group = heads // SIDE
    step = 32

    def taken(partner):
        return pl.BlockSpec((step, group, width), lambda i, s: (i, s[0] ^ partner, 0))

    sizes = [3 * group] * SIDE + [group // WAVES] * (SIDE * WAVES)
    return pl.pallas_call(
        pack_kernel,
        grid_spec=pltpu.PrefetchScalarGridSpec(
            num_scalar_prefetch=1,
            grid=(rows // step,),
            in_specs=[taken(partner) for partner in range(SIDE) for _ in range(3)],
            out_specs=[pl.BlockSpec((n, step, width), lambda i, s: (0, i, 0)) for n in sizes],
        ),
        out_shape=[jax.ShapeDtypeStruct((n, rows, width), bf16) for n in sizes],
        compiler_params=pltpu.CompilerParams(vmem_limit_bytes=VMEM),
        name="pack",
    )(side, *([queries, keys, values] * SIDE))


def pack_context_kernel(*refs):
    sources, outs = refs[1 : 1 + 2 * SIDE], refs[1 + 2 * SIDE :]
    part = outs[0].shape[0]
    start = refs[0][1] * part
    for partner in range(SIDE):
        for which in range(2):
            x = sources[2 * partner + which]
            for head in range(part):
                outs[partner][head, which] = x[:, pl.ds(start + head, 1), :][:, 0, :].astype(bf16)


def pack_context(keys, values, side, part):
    rows, heads, width = keys.shape
    group = heads // SIDE

    def taken(partner):
        return pl.BlockSpec((rows, group, width), lambda i, s: (0, s[0] ^ partner, 0))

    shape = (part, 2, rows, width)
    return pl.pallas_call(
        pack_context_kernel,
        grid_spec=pltpu.PrefetchScalarGridSpec(
            num_scalar_prefetch=1,
            grid=(1,),
            in_specs=[taken(partner) for partner in range(SIDE) for _ in range(2)],
            out_specs=[pl.BlockSpec(shape, lambda i, s: (0, 0, 0, 0))] * SIDE,
        ),
        out_shape=[jax.ShapeDtypeStruct(shape, bf16)] * SIDE,
        compiler_params=pltpu.CompilerParams(vmem_limit_bytes=VMEM),
        name="pack_context",
    )(side, *([keys.astype(f32), values.astype(f32)] * SIDE))


def softmax_columns(pieces, scaling):
    highest = functools.reduce(jnp.maximum, [jnp.max(s, axis=0, keepdims=True) for s, _ in pieces])
    total = mixed = 0.0
    for scores, values in pieces:
        weights = jnp.exp((scores - highest) * scaling)
        total += jnp.sum(weights, axis=0, keepdims=True)
        mixed += lax.dot_general(values, weights.astype(bf16), (((0,), (0,)), ((), ())), preferred_element_type=f32)
    return mixed / total, highest * scaling + jnp.log(total)


def thirds(x):
    first = x.astype(bf16).astype(f32)
    second = (x - first).astype(bf16).astype(f32)
    return first, second, x - first - second


def products(keys, queries):
    return lax.dot_general(keys, queries, (((1,), (1,)), ((), ())), preferred_element_type=f32)


def visit_kernel(wave, side_ref, *refs):
    q_refs, kv_refs, outs = refs[:SIDE], refs[SIDE : 2 * SIDE], refs[2 * SIDE :]
    each, rows, width = q_refs[0].shape
    group = kv_refs[0].shape[0] // 3
    scaling = 1.0 / math.sqrt(width)

    @pl.when(side_ref[2] == 0)
    def _():
        stats = [[], [], []]
        for head in range(each):
            place = wave * each + head
            queries = jnp.concatenate([q[head] for q in q_refs], axis=0)
            keys = jnp.concatenate([r[group + place] for r in kv_refs], axis=0)
            values = jnp.concatenate([r[2 * group + place] for r in kv_refs], axis=0)
            mixed, level = softmax_columns([(products(keys, queries), values)], scaling)
            result = mixed.T.astype(bf16)
            for partner in range(SIDE):
                outs[partner][head * rows : (head + 1) * rows] = result[partner * rows : (partner + 1) * rows]
            for third, value in enumerate(thirds(level)):
                stats[third].append(value)
        pad = outs[0].shape[0] - each * rows - 3 * each
        lines = stats[0] + stats[1] + stats[2]
        if pad > 0:
            lines.append(jnp.zeros((pad, SIDE * rows), f32))
        block = jnp.concatenate(lines, axis=0).astype(bf16)
        for partner in range(SIDE):
            outs[partner][each * rows :] = block[:, partner * rows : (partner + 1) * rows]


def stat_rows(heads):
    return -(-3 * heads // 16) * 16


def visit(wave, queries, packs, side):
    each, rows, width = queries[0].shape
    out = (each * rows + stat_rows(each), width)
    pairs = each * (SIDE * rows) ** 2
    whole = pl.BlockSpec(memory_space=pltpu.VMEM)
    return pl.pallas_call(
        functools.partial(visit_kernel, wave),
        in_specs=[pl.BlockSpec(memory_space=pltpu.SMEM)] + [whole] * (2 * SIDE),
        out_specs=[whole] * SIDE,
        out_shape=[jax.ShapeDtypeStruct(out, bf16)] * SIDE,
        cost_estimate=pl.CostEstimate(flops=4 * pairs * width, bytes_accessed=4 << 20, transcendentals=pairs),
        compiler_params=pltpu.CompilerParams(vmem_limit_bytes=VMEM),
        name="visit",
    )(side, *queries, *packs)


def own_kernel(parts, side_ref, *refs):
    qkv_refs, refs = refs[: 3 * SIDE], refs[3 * SIDE :]
    context_refs, refs = refs[:parts], refs[parts:]
    outs, (qs, ks, vs, os, ck, cv, level_ref, stat_ref) = refs[:SIDE], refs[SIDE:]
    _, rows, width = qkv_refs[0].shape
    side = side_ref[0]
    step = pl.program_id(0)
    each = context_refs[0].shape[1]
    group = pl.num_programs(0)
    head = ((step // each) ^ side_ref[1]) * each + step % each
    scaling = 1.0 / math.sqrt(width)
    length = SIDE * rows

    for partner in range(SIDE):
        place = pl.ds(pl.multiple_of((side ^ partner) * rows, rows), rows)
        qs[place] = qkv_refs[3 * partner][0]
        ks[place] = qkv_refs[3 * partner + 1][0]
        vs[place] = qkv_refs[3 * partner + 2][0]
    for part in range(parts):

        @pl.when(step // each == part)
        def _():
            ck[...] = context_refs[part][:, pl.ds(step % each, 1), 0].reshape(ck.shape)
            cv[...] = context_refs[part][:, pl.ds(step % each, 1), 1].reshape(cv.shape)

    block = 2 * rows
    for index in range(length // block):
        here = slice(index * block, (index + 1) * block)
        queries = qs[here]
        pieces = [(products(ck[...], queries), cv[...])]
        if index > 0:
            pieces.append((products(ks[: index * block], queries), vs[: index * block]))
        scores = products(ks[here], queries)
        allowed = lax.broadcasted_iota(jnp.int32, scores.shape, 0) <= lax.broadcasted_iota(jnp.int32, scores.shape, 1)
        pieces.append((jnp.where(allowed, scores, masked_score), vs[here]))
        mixed, level = softmax_columns(pieces, scaling)
        os[here] = mixed.T.astype(bf16)
        for part in range(block // rows):
            level_ref[index * (block // rows) + part, 0:1] = level[:, part * rows : (part + 1) * rows]
    at = pl.ds(pl.multiple_of(head * rows, rows), rows)
    for partner in range(SIDE):
        place = side ^ partner
        outs[partner][at] = os[pl.ds(pl.multiple_of(place * rows, rows), rows)]
        for third, value in enumerate(thirds(level_ref[place, 0:1])):
            stat_ref[partner, pl.ds(third * group + head, 1)] = value

    @pl.when(step == group - 1)
    def _():
        for partner in range(SIDE):
            outs[partner][group * rows :] = stat_ref[partner].astype(bf16)


def own(packs, contexts, side):
    triple, rows, width = packs[0].shape
    group = triple // 3
    parts = len(contexts)
    each = contexts[0].shape[1]
    sources, context_rows = contexts[0].shape[0], contexts[0].shape[3]
    stats = stat_rows(group)

    def taken(which):
        return pl.BlockSpec(
            (1, rows, width), lambda i, s: (which * group + ((i // each) ^ s[1]) * each + i % each, 0, 0)
        )

    def whole(shape):
        return pl.BlockSpec(shape, lambda i, s: (0,) * len(shape))

    out = (group * rows + stats, width)
    pairs = group * SIDE * rows * (sources * context_rows + SIDE * rows * 3 // 4)
    operands = [p for p in packs for _ in range(3)]
    return pl.pallas_call(
        functools.partial(own_kernel, parts),
        grid_spec=pltpu.PrefetchScalarGridSpec(
            num_scalar_prefetch=1,
            grid=(group,),
            in_specs=[taken(which) for _ in packs for which in range(3)] + [whole(c.shape) for c in contexts],
            out_specs=[whole(out)] * SIDE,
            scratch_shapes=[pltpu.VMEM((SIDE * rows, width), bf16)] * 4
            + [pltpu.VMEM((sources * context_rows, width), bf16)] * 2
            + [pltpu.VMEM((SIDE, 8, rows), f32), pltpu.VMEM((SIDE, stats, rows), f32)],
        ),
        out_shape=[jax.ShapeDtypeStruct(out, bf16)] * SIDE,
        cost_estimate=pl.CostEstimate(flops=4 * pairs * width, bytes_accessed=10 << 20, transcendentals=pairs),
        compiler_params=pltpu.CompilerParams(vmem_limit_bytes=VMEM),
        name="own",
    )(side, *operands, *contexts)


def merge_kernel(side_ref, *refs):
    mine, visits, out = refs[:SIDE], refs[SIDE : SIDE + SIDE * WAVES], refs[-1]
    step, group, width = out.shape
    rows = mine[0].shape[1]
    each = group // WAVES
    second = jnp.full((rows, group), side_ref[2], jnp.int32) == 1
    place = lax.broadcasted_iota(jnp.int32, (step, group, width), 0)

    def levels(ref, heads):
        lines = ref[heads * rows : heads * rows + stat_rows(heads)].astype(f32)
        return lines[:heads] + lines[heads : 2 * heads] + lines[2 * heads : 3 * heads]

    for partner in range(SIDE):

        @pl.when(pl.program_id(0) == partner)
        def _():
            here = levels(mine[partner], group)
            there = jnp.concatenate([levels(visits[w * SIDE + partner], each) for w in range(WAVES)], axis=0)
            gap = (there - here).T
            first_share = jnp.where(second, 1.0 / (1.0 + jnp.exp(gap)), 1.0)
            other_share = jnp.where(second, 1.0 / (1.0 + jnp.exp(-gap)), 0.0)
            heads = []
            for head in range(group):
                a = mine[partner][head * rows : (head + 1) * rows].astype(f32)
                local = head % each
                b = visits[head // each * SIDE + partner][local * rows : (local + 1) * rows].astype(f32)
                heads.append(a * first_share[:, head : head + 1] + b * other_share[:, head : head + 1])
            result = jnp.transpose(jnp.stack(heads), (1, 0, 2))
            out[...] = jnp.where(place < side_ref[3], result, 0.0).astype(bf16)


def merge(mine, visits, side, heads):
    rows = mine[0].shape[1]
    width = mine[0].shape[1]
    group = heads // SIDE

    def whole(x):
        return pl.BlockSpec(x.shape, lambda i, s: (0, 0))

    return pl.pallas_call(
        merge_kernel,
        grid_spec=pltpu.PrefetchScalarGridSpec(
            num_scalar_prefetch=1,
            grid=(SIDE,),
            in_specs=[whole(x) for x in (*mine, *visits)],
            out_specs=pl.BlockSpec((rows, group, width), lambda i, s: (0, s[0] ^ i, 0)),
        ),
        out_shape=jax.ShapeDtypeStruct((rows, heads, width), bf16),
        compiler_params=pltpu.CompilerParams(vmem_limit_bytes=VMEM),
        name="merge",
    )(side, *mine, *visits)


def attention_by_halves(cont_queries, cont_keys, cont_values, context_keys, context_values, left):
    heads = cont_queries.shape[1]
    cands = lax.axis_size("cand")
    me, mine = lax.axis_index("seq"), lax.axis_index("cand")
    peers = 2 * SIDE
    side = jnp.stack([me % SIDE, mine, me // SIDE, left]).astype(jnp.int32)

    def within(x, k):
        return lax.ppermute(x, "seq", [(i, i ^ k) for i in range(peers)])

    def down(x, k):
        return lax.ppermute(x, "seq", [(i, i ^ (SIDE + k)) for i in range(SIDE, peers)])

    def up(x, k):
        return lax.ppermute(x, "seq", [(i, i ^ (SIDE + k)) for i in range(SIDE)])

    def swap(x, k):
        return lax.ppermute(x, "cand", [(i, i ^ k) for i in range(cands)])

    packed = pack(cont_queries, cont_keys, cont_values, side)
    own_packs, crossing = packed[:SIDE], packed[SIDE:]
    visitors = [[down(crossing[w * SIDE + k], k) for k in range(SIDE)] for w in range(WAVES)]
    packs = [own_packs[0]] + [within(own_packs[k], k) for k in range(1, SIDE)]

    part = heads // SIDE // cands
    sent = pack_context(context_keys, context_values, side, part)
    context = jnp.stack([within(sent[k % SIDE], k) if k else sent[0] for k in range(peers)])
    across = swap(context, 2)
    contexts = [context, swap(context, 1), across, swap(across, 1)]

    visits = []
    for w in range(WAVES):
        parts = visit(w, visitors[w], packs, side)
        visits += [up(parts[k], k) for k in range(SIDE)]
    results = own(packs, contexts, side)
    results = [results[0]] + [within(results[k], k) for k in range(1, SIDE)]
    return merge(results, visits, side, heads)


def local(
    hyena_query,
    hyena_key,
    hyena_value,
    hyena_filters,
    context_tail,
    cont_queries,
    cont_keys,
    cont_values,
    context_keys,
    context_values,
    lengths,
):
    peers = lax.axis_size("seq")
    me = lax.axis_index("seq")
    rows = hyena_key.shape[1]
    heads = cont_queries.shape[2]
    left = (lengths[0] - me * rows).astype(jnp.int32)

    product = (hyena_key[0].astype(f32) * hyena_value[0].astype(f32)).astype(bf16)
    received = lax.ppermute(product, "seq", [(i, i + 1) for i in range(peers - 1)])
    place = jnp.stack([me.astype(jnp.int32), left])

    halves = peers == 2 * SIDE and lax.axis_size("cand") == 4 and heads % 32 == 0 and rows == LANES
    attention = attention_by_halves if halves else attention_by_heads
    attention_out = attention(
        cont_queries[0], cont_keys[0], cont_values[0], context_keys, context_values, left
    )[None]
    hyena_out = hyena(hyena_query, hyena_key, hyena_value, received, context_tail, hyena_filters, place)
    return (hyena_out, attention_out)


def solution(mesh):
    placed = (
        P("cand", "seq", None),
        P("cand", "seq", None),
        P("cand", "seq", None),
        P(),
        P(),
        P("cand", "seq", None, None),
        P("cand", "seq", None, None),
        P("cand", "seq", None, None),
        P("seq", None, None),
        P("seq", None, None),
        P("cand"),
    )
    return jax.shard_map(
        local,
        mesh=mesh,
        in_specs=placed,
        out_specs=(P("cand", "seq", None), P("cand", "seq", None, None)),
        check_vma=False,
    )
```

```python
import functools
import math

import jax
import jax.numpy as jnp
from jax import lax
from jax.experimental import pallas as pl
from jax.experimental.pallas import tpu as pltpu
from jax.sharding import PartitionSpec as P

CH_GROUP = 16
LANES = 128
VMEM = 56 * 1024 * 1024
WAVES = 2
SIDE = 4
BLOCK = 256
EARLY = 2

masked_score = -1e30
TINY = pl.CostEstimate(flops=1, bytes_accessed=1, transcendentals=0)

bf16 = jnp.bfloat16
f32 = jnp.float32


def hyena_kernel(place_ref, query_ref, key_ref, value_ref, near_ref, even_ref, odd_ref, tail_ref, wave_ref, *refs):
    rows, lanes = key_ref.shape[1], key_ref.shape[2]
    out_ref = refs[-1]
    groups = LANES // CH_GROUP
    product = (key_ref[0].astype(f32) * value_ref[0].astype(f32)).astype(bf16)
    shape = (rows, lanes)
    first = jnp.broadcast_to(place_ref[0], shape) == 0
    even = jnp.broadcast_to(place_ref[0] % 2, shape) == 0
    lower = jnp.broadcast_to(pl.program_id(0), shape) < pl.num_programs(0) // 2
    earlier = jnp.where(even, even_ref[...].astype(f32), odd_ref[...].astype(f32))
    earlier = jnp.where(lower, near_ref[...].astype(f32), earlier)
    earlier = jnp.where(first, tail_ref[...].astype(f32), earlier)
    extended = jnp.concatenate([earlier.astype(bf16), product], axis=0)
    channel = lax.broadcasted_iota(jnp.int32, (rows, LANES), 1) // CH_GROUP
    tiles = []
    for tile in range(lanes // LANES):
        columns = extended[:, tile * LANES : (tile + 1) * LANES]
        convolved = jnp.zeros((rows, LANES), f32)
        for group in range(groups):
            line = tile * groups + group
            wave = jnp.broadcast_to(wave_ref[line : line + 1, :], (rows, 2 * rows))
            taps = pltpu.roll(wave, 0, 1, stride=1, stride_axis=0)
            high = taps.astype(bf16)
            low = (taps - high.astype(f32)).astype(bf16)
            term = jnp.dot(high, columns, preferred_element_type=f32) + jnp.dot(
                low, columns, preferred_element_type=f32
            )
            convolved = jnp.where(channel == group, term, convolved)
        tiles.append(convolved)
    convolved = jnp.concatenate(tiles, axis=1)
    places = lax.broadcasted_iota(jnp.int32, (rows, lanes), 0)
    gated = query_ref[0].astype(f32) * convolved
    out_ref[0] = jnp.where(places < place_ref[1], gated, 0.0).astype(bf16)


def hyena(query, key, value, received, constants, place, after):
    _, rows, channels = key.shape
    wave, tail = constants
    groups = LANES // CH_GROUP
    lanes = math.gcd(channels // 2, 8 * LANES)
    steps = channels // lanes // 2
    block = pl.BlockSpec((1, rows, lanes), lambda i: (0, 0, i))
    flat = pl.BlockSpec((rows, lanes), lambda i: (0, i))
    return pl.pallas_call(
        hyena_kernel,
        grid=(channels // lanes,),
        out_shape=jax.ShapeDtypeStruct(query.shape, bf16),
        in_specs=[
            pl.BlockSpec(memory_space=pltpu.SMEM),
            block,
            block,
            block,
            pl.BlockSpec((rows, lanes), lambda i: (0, jnp.minimum(i, steps - 1))),
            pl.BlockSpec((rows, lanes), lambda i: (0, jnp.maximum(i - steps, 0))),
            pl.BlockSpec((rows, lanes), lambda i: (0, jnp.maximum(i - steps, 0))),
            flat,
            pl.BlockSpec((lanes // CH_GROUP, 2 * rows), lambda i: (i, 0)),
        ]
        + [pl.BlockSpec(memory_space=pl.ANY)] * len(after),
        out_specs=block,
        cost_estimate=TINY,
        name="hyena",
    )(place, query, key, value, *received, tail, wave, *after)


def attend_kernel(block_rows, q_ref, k_ref, v_ref, ck_ref, cv_ref, out_ref):
    sources, _, rows, width = k_ref.shape
    index = pl.program_id(1)
    scaling = 1.0 / math.sqrt(width)
    context = ck_ref.shape[1] * ck_ref.shape[3]
    contract = (((1,), (1,)), ((), ()))
    queries = q_ref[...].reshape(block_rows, width)
    per = block_rows // rows

    def fold(carried, scores, values):
        run_max, run_total, mixed = carried
        highest = jnp.maximum(run_max, jnp.max(scores, axis=1, keepdims=True))
        weights = jnp.exp((scores - highest) * scaling)
        shrink = jnp.exp((run_max - highest) * scaling)
        total = run_total * shrink + jnp.sum(weights, axis=1, keepdims=True)
        mixed = mixed * shrink + jnp.dot(weights.astype(bf16), values, preferred_element_type=f32)
        return highest, total, mixed

    def own(block):
        keys = k_ref[pl.ds(block * per, per), 0].reshape(block_rows, width)
        values = v_ref[pl.ds(block * per, per), 0].reshape(block_rows, width)
        return lax.dot_general(queries, keys, contract, preferred_element_type=f32), values

    scores, values = own(index)
    shape = (block_rows, block_rows)
    allowed = lax.broadcasted_iota(jnp.int32, shape, 1) <= lax.broadcasted_iota(jnp.int32, shape, 0)
    scores = jnp.where(allowed, scores, masked_score)
    start = (
        jnp.full((block_rows, 1), masked_score, f32),
        jnp.zeros((block_rows, 1), f32),
        jnp.zeros((block_rows, width), f32),
    )
    carried = fold(start, scores, values)
    carried = lax.fori_loop(0, index, lambda i, c: fold(c, *own(i)), carried)
    context_keys = ck_ref[0, :, 0].reshape(context, width)
    context_values = cv_ref[0, :, 0].reshape(context, width)
    scores = lax.dot_general(queries, context_keys, contract, preferred_element_type=f32)
    _, total, mixed = fold(carried, scores, context_values)
    out_ref[...] = (mixed / total).astype(bf16).reshape(out_ref.shape)


def attend(queries, keys, values, context):
    sources, heads, rows, width = queries.shape
    per = 2 if sources % 2 == 0 else 1
    whole = pl.BlockSpec((sources, 1, rows, width), lambda h, i: (0, h, 0, 0))
    part = pl.BlockSpec((per, 1, rows, width), lambda h, i: (i, h, 0, 0))

    def shared(which):
        return pl.BlockSpec((1, context.shape[1], 1) + context.shape[3:], lambda h, i: (h, 0, which, 0, 0))

    length, context_rows = sources * rows, context.shape[1] * context.shape[3]
    pairs = heads * length * (context_rows + (length + rows * per) // 2)
    return pl.pallas_call(
        functools.partial(attend_kernel, rows * per),
        grid=(heads, sources // per),
        out_shape=jax.ShapeDtypeStruct(queries.shape, bf16),
        in_specs=[part, whole, whole, shared(0), shared(1)],
        out_specs=part,
        cost_estimate=TINY,
        compiler_params=pltpu.CompilerParams(vmem_limit_bytes=VMEM),
        name="attend",
    )(queries, keys, values, context, context)


def attention_by_heads(cont_queries, cont_keys, cont_values, context_keys, context_values, left):
    peers = lax.axis_size("seq")
    rows, heads, width = cont_queries.shape
    share = heads // peers

    def by_owner(x):
        return x.reshape(x.shape[0], peers, share, width).transpose(1, 2, 0, 3)

    def exchange(x):
        return lax.all_to_all(x, "seq", split_axis=0, concat_axis=0, tiled=True)

    pair = exchange(jnp.stack([by_owner(context_keys), by_owner(context_values)], axis=2))
    context = pair.transpose(1, 0, 2, 3, 4)
    queries = exchange(by_owner(cont_queries))
    keys = exchange(by_owner(cont_keys))
    values = exchange(by_owner(cont_values))
    attended = exchange(attend(queries, keys, values, context))
    attention = attended.transpose(2, 0, 1, 3).reshape(rows, heads, width)
    keep = jnp.arange(rows)[:, None, None] < left
    return jnp.where(keep, attention, jnp.zeros((), bf16))


def pack_kernel(peers, side_ref, *refs):
    sources, outs, (heads_first, context_first) = refs[:5], refs[5:-2], refs[-2:]
    rows, heads, _ = sources[0].shape
    share = heads // peers
    each = share // WAVES
    for which, ref in enumerate(sources[:3]):
        heads_first[...] = jnp.transpose(ref[...], (1, 0, 2))
        for index, out in enumerate(outs):
            wave, partner = divmod(index, peers)
            start = (side_ref[2] ^ partner) * share + wave * each
            taken = heads_first[pl.ds(start, each)]
            for head in range(each):
                at = (which * each + head) * rows
                out[at : at + rows] = taken[head]
    for which, ref in enumerate(sources[3:]):
        context_first[...] = jnp.transpose(ref[...], (1, 0, 2))
        for partner, out in enumerate(outs[:peers]):
            start = (side_ref[2] ^ partner) * share + side_ref[1]
            at = 3 * each * rows + which * ref.shape[0]
            out[at : at + ref.shape[0]] = context_first[pl.ds(start, 1)][0]


def pack(arrays, side, peers):
    rows, heads, width = arrays[0].shape
    context_rows = arrays[3].shape[0]
    size = 3 * heads // peers // WAVES * rows
    sizes = [size + 2 * context_rows] * peers + [size] * (peers * (WAVES - 1))
    packed = pl.pallas_call(
        functools.partial(pack_kernel, peers),
        grid_spec=pltpu.PrefetchScalarGridSpec(
            num_scalar_prefetch=1,
            grid=(1,),
            in_specs=[pl.BlockSpec(x.shape, lambda i, s: (0, 0, 0)) for x in arrays],
            out_specs=[pl.BlockSpec((n, width), lambda i, s: (0, 0)) for n in sizes],
            scratch_shapes=[pltpu.VMEM((heads, rows, width), bf16), pltpu.VMEM((heads, context_rows, width), bf16)],
        ),
        out_shape=[jax.ShapeDtypeStruct((n, width), bf16) for n in sizes],
        cost_estimate=TINY,
        compiler_params=pltpu.CompilerParams(vmem_limit_bytes=VMEM),
        name="pack",
    )(side, *arrays)
    return [list(packed[wave * peers : (wave + 1) * peers]) for wave in range(WAVES)]


def gate_kernel(*refs):
    pass


def gate(x, after):
    anywhere = pl.BlockSpec(memory_space=pl.ANY)
    return pl.pallas_call(
        gate_kernel,
        in_specs=[anywhere] * (1 + len(after)),
        out_specs=anywhere,
        out_shape=jax.ShapeDtypeStruct(x.shape, x.dtype),
        input_output_aliases={0: 0},
        cost_estimate=TINY,
        name="gate",
    )(x, *after)


def gather_kernel(*refs):
    for index in range(refs[-1].shape[0]):
        refs[-1][index] = refs[index][...]


def gather(arrays, size, after):
    last = arrays[0].shape[0] // size - 1
    shape = (len(arrays), size, arrays[0].shape[1])
    return pl.pallas_call(
        gather_kernel,
        grid=(1,),
        in_specs=[pl.BlockSpec(shape[1:], lambda i: (last, 0))] * len(arrays)
        + [pl.BlockSpec(memory_space=pl.ANY)] * len(after),
        out_specs=pl.BlockSpec(shape, lambda i: (0, 0, 0)),
        out_shape=jax.ShapeDtypeStruct(shape, bf16),
        cost_estimate=TINY,
        name="gather",
    )(*arrays, *after)


def softmax_columns(pieces, scaling):
    highest = functools.reduce(jnp.maximum, [jnp.max(s, axis=0, keepdims=True) for s, _ in pieces])
    total = mixed = 0.0
    for scores, values in pieces:
        weights = jnp.exp((scores - highest) * scaling)
        total += jnp.sum(weights, axis=0, keepdims=True)
        mixed += lax.dot_general(values, weights.astype(bf16), (((0,), (0,)), ((), ())), preferred_element_type=f32)
    return mixed / total


def products(keys, queries):
    return lax.dot_general(keys, queries, (((1,), (1,)), ((), ())), preferred_element_type=f32)


def wave_kernel(wave, peers, side_ref, *refs):
    arrived, contexts, refs = refs[: 3 * peers], refs[3 * peers : 3 * peers + SIDE], refs[-peers - 6 :]
    outs, (qs, ks, vs, os, slots, sems) = refs[:peers], refs[peers:]
    rows, width = arrived[0].shape
    step = pl.program_id(0)
    each = slots.shape[0]
    scaling = 1.0 / math.sqrt(width)
    context_rows = slots.shape[2] // 2

    def each_copy(head, act):
        part = (wave * each + head) ^ side_ref[1]
        for number in range(SIDE):

            @pl.when(part == number)
            def _():
                act(pltpu.make_async_copy(contexts[number], slots.at[head], sems.at[head]))

    @pl.when(step == 0)
    def _():
        for head in range(each):
            each_copy(head, lambda copy: copy.start())

    places = [pl.ds(pl.multiple_of((side_ref[2] ^ partner) * rows, rows), rows) for partner in range(peers)]
    for partner, place in enumerate(places):
        qs[place] = arrived[3 * partner][...]
        ks[place] = arrived[3 * partner + 1][...]
        vs[place] = arrived[3 * partner + 2][...]

    for head in range(each):

        @pl.when(step == head)
        def _():
            each_copy(head, lambda copy: copy.wait())

    context_keys = slots[step, :, :context_rows].reshape(peers * context_rows, width)
    context_values = slots[step, :, context_rows:].reshape(peers * context_rows, width)
    block = min(BLOCK, peers * rows)
    for index in range(peers * rows // block):
        here = slice(index * block, (index + 1) * block)
        queries = qs[here]
        pieces = [(products(context_keys, queries), context_values)]
        if index > 0:
            before = slice(0, index * block)
            pieces.append((products(ks[before], queries), vs[before]))
        scores = products(ks[here], queries)
        allowed = lax.broadcasted_iota(jnp.int32, scores.shape, 0) <= lax.broadcasted_iota(
            jnp.int32, scores.shape, 1
        )
        pieces.append((jnp.where(allowed, scores, masked_score), vs[here]))
        os[here] = softmax_columns(pieces, scaling).T.astype(bf16)
    for partner, place in enumerate(places):
        outs[partner][0] = os[place]


def attend_wave(wave, arrived, contexts, side, after):
    peers = len(arrived)
    rows, width = LANES, arrived[0].shape[1]
    each = arrived[0].shape[0] // rows // 3

    def taken(which):
        return pl.BlockSpec((rows, width), lambda i, s: (which * each + i, 0))

    result = pl.BlockSpec((1, rows, width), lambda i, s: (i, 0, 0))
    return pl.pallas_call(
        functools.partial(wave_kernel, wave, peers),
        grid_spec=pltpu.PrefetchScalarGridSpec(
            num_scalar_prefetch=1,
            grid=(each,),
            in_specs=[taken(which) for _ in arrived for which in range(3)]
            + [pl.BlockSpec(memory_space=pl.ANY)] * (SIDE + len(after)),
            out_specs=[result] * peers,
            scratch_shapes=[pltpu.VMEM((peers * rows, width), bf16)] * 4
            + [pltpu.VMEM((each,) + contexts[0].shape, bf16), pltpu.SemaphoreType.DMA((each,))],
        ),
        out_shape=[jax.ShapeDtypeStruct((each, rows, width), bf16)] * peers,
        cost_estimate=TINY,
        compiler_params=pltpu.CompilerParams(vmem_limit_bytes=VMEM),
        name="attend_wave",
    )(side, *[x for x in arrived for _ in range(3)], *contexts, *after)


def unpack_kernel(peers, side_ref, *refs):
    arrived, (out, heads_first) = refs[:-2], refs[-2:]
    each = arrived[0].shape[0]
    for index, ref in enumerate(arrived):
        wave, partner = divmod(index, peers)
        heads_first[pl.ds((side_ref[2] ^ partner) * each * WAVES + wave * each, each)] = ref[...].astype(f32)
    result = jnp.transpose(heads_first[...], (1, 0, 2))
    place = lax.broadcasted_iota(jnp.int32, result.shape, 0) + pl.program_id(0) * result.shape[0]
    out[...] = jnp.where(place < side_ref[0], result, 0.0).astype(bf16)


def unpack(arrived, side):
    each, rows, width = arrived[0].shape
    heads = each * len(arrived)
    step = rows // 4
    return pl.pallas_call(
        functools.partial(unpack_kernel, len(arrived) // WAVES),
        grid_spec=pltpu.PrefetchScalarGridSpec(
            num_scalar_prefetch=1,
            grid=(rows // step,),
            in_specs=[pl.BlockSpec((each, step, width), lambda i, s: (0, i, 0))] * len(arrived),
            out_specs=pl.BlockSpec((step, heads, width), lambda i, s: (i, 0, 0)),
            scratch_shapes=[pltpu.VMEM((heads, step, width), f32)],
        ),
        out_shape=jax.ShapeDtypeStruct((rows, heads, width), bf16),
        cost_estimate=TINY,
        compiler_params=pltpu.CompilerParams(vmem_limit_bytes=VMEM),
        name="unpack",
    )(side, *arrived)


def in_waves(arrays, left, key, value, constants, finish):
    peers = lax.axis_size("seq")
    cands = lax.axis_size("cand")
    side = jnp.stack([left, lax.axis_index("cand"), lax.axis_index("seq")]).astype(jnp.int32)

    def exchange(parts, chosen):
        parts = list(parts)
        for k in chosen:
            parts[k] = lax.ppermute(parts[k], "seq", [(i, i ^ k) for i in range(peers)])
        return parts

    def swap(x, k):
        return lax.ppermute(x, "cand", [(i, i ^ k) for i in range(cands)])

    everyone, near_by, across_half = range(1, peers), range(1, peers // 2), range(peers // 2, peers)
    one, two = pack(arrays, side, peers)
    one = exchange(one, everyone)
    two = exchange(two, across_half)
    received = brought((key.astype(f32) * value.astype(f32)).astype(bf16))
    context = gather(one, 2 * arrays[3].shape[0], constants)
    across = swap(context, 2)
    contexts = [context, swap(context, 1), across, swap(across, 1)]

    first = attend_wave(0, one, contexts, side, tuple(two[k] for k in across_half[:EARLY]))
    two = [gate(x, (first[0],)) if k in near_by else x for k, x in enumerate(two)]
    two = exchange(two, near_by)
    hyena_out = finish(received, (first[0],))
    second = attend_wave(1, two, contexts, side, (hyena_out,))
    return unpack(exchange(first, everyone) + exchange(second, everyone), side), hyena_out


def brought(product):
    peers = lax.axis_size("seq")
    half = product.shape[1] // 2
    near, far = product[:, :half], product[:, half:]
    near = lax.ppermute(near, "seq", [(i, i + 1) for i in range(peers - 1)])
    odd = lax.ppermute(far, "seq", [(i, i ^ 1) for i in range(peers)])
    even = lax.ppermute(odd, "seq", [(i, i + 2) for i in range(0, peers - 2, 2)])
    return near, even, odd


def local(
    hyena_query,
    hyena_key,
    hyena_value,
    hyena_filters,
    context_tail,
    cont_queries,
    cont_keys,
    cont_values,
    context_keys,
    context_values,
    lengths,
):
    peers = lax.axis_size("seq")
    me = lax.axis_index("seq")
    rows = hyena_key.shape[1]
    heads = cont_queries.shape[2]
    left = (lengths[0] - me * rows).astype(jnp.int32)

    place = jnp.stack([me.astype(jnp.int32), left])

    wave = jnp.pad(hyena_filters[::-1], ((1, 2 * rows - hyena_filters.shape[0] - 1), (0, 0))).T
    constants = (wave, jnp.pad(context_tail, ((1, 0), (0, 0))))

    def finish(received, after):
        return hyena(hyena_query, hyena_key, hyena_value, received, constants, place, after)

    share = heads // peers
    waves = share == SIDE and lax.axis_size("cand") == SIDE and peers & (peers - 1) == 0
    arrays = (cont_queries[0], cont_keys[0], cont_values[0], context_keys, context_values)
    key, value = hyena_key[0], hyena_value[0]
    if waves:
        attention_out, hyena_out = in_waves(arrays, left, key, value, constants, finish)
    else:
        attention_out = attention_by_heads(*arrays, left)
        hyena_out = finish(brought((key.astype(f32) * value.astype(f32)).astype(bf16)), ())
    return (hyena_out, attention_out[None])


def solution(mesh):
    placed = (
        P("cand", "seq", None),
        P("cand", "seq", None),
        P("cand", "seq", None),
        P(),
        P(),
        P("cand", "seq", None, None),
        P("cand", "seq", None, None),
        P("cand", "seq", None, None),
        P("seq", None, None),
        P("seq", None, None),
        P("cand"),
    )
    return jax.shard_map(
        local,
        mesh=mesh,
        in_specs=placed,
        out_specs=(P("cand", "seq", None), P("cand", "seq", None, None)),
        check_vma=False,
    )
```

```python
import functools
import math

import jax
import jax.numpy as jnp
from jax import lax
from jax.experimental import pallas as pl
from jax.experimental.pallas import tpu as pltpu
from jax.sharding import PartitionSpec as P

CH_GROUP = 16
LANES = 128
VMEM = 56 * 1024 * 1024
WAVES = 2
SIDE = 4
BLOCK = 512
EARLY = 2

masked_score = -1e30
TINY = pl.CostEstimate(flops=1, bytes_accessed=1, transcendentals=0)

bf16 = jnp.bfloat16
f32 = jnp.float32


def hyena_kernel(place_ref, query_ref, key_ref, value_ref, near_ref, even_ref, odd_ref, tail_ref, wave_ref, *refs):
    rows, lanes = key_ref.shape[1], key_ref.shape[2]
    out_ref = refs[-1]
    groups = LANES // CH_GROUP
    product = (key_ref[0].astype(f32) * value_ref[0].astype(f32)).astype(bf16)
    shape = (rows, lanes)
    first = jnp.broadcast_to(place_ref[0], shape) == 0
    even = jnp.broadcast_to(place_ref[0] % 2, shape) == 0
    lower = jnp.broadcast_to(pl.program_id(0), shape) < pl.num_programs(0) // 2
    earlier = jnp.where(even, even_ref[...].astype(f32), odd_ref[...].astype(f32))
    earlier = jnp.where(lower, near_ref[...].astype(f32), earlier)
    earlier = jnp.where(first, tail_ref[...].astype(f32), earlier)
    extended = jnp.concatenate([earlier.astype(bf16), product], axis=0)
    channel = lax.broadcasted_iota(jnp.int32, (rows, LANES), 1) // CH_GROUP
    tiles = []
    for tile in range(lanes // LANES):
        columns = extended[:, tile * LANES : (tile + 1) * LANES]
        convolved = jnp.zeros((rows, LANES), f32)
        for group in range(groups):
            line = tile * groups + group
            wave = jnp.broadcast_to(wave_ref[line : line + 1, :], (rows, 2 * rows))
            taps = pltpu.roll(wave, 0, 1, stride=1, stride_axis=0)
            high = taps.astype(bf16)
            low = (taps - high.astype(f32)).astype(bf16)
            term = jnp.dot(high, columns, preferred_element_type=f32) + jnp.dot(
                low, columns, preferred_element_type=f32
            )
            convolved = jnp.where(channel == group, term, convolved)
        tiles.append(convolved)
    convolved = jnp.concatenate(tiles, axis=1)
    places = lax.broadcasted_iota(jnp.int32, (rows, lanes), 0)
    gated = query_ref[0].astype(f32) * convolved
    out_ref[0] = jnp.where(places < place_ref[1], gated, 0.0).astype(bf16)


def hyena(query, key, value, received, constants, place, after):
    _, rows, channels = key.shape
    wave, tail = constants
    groups = LANES // CH_GROUP
    lanes = math.gcd(channels // 2, 8 * LANES)
    steps = channels // lanes // 2
    block = pl.BlockSpec((1, rows, lanes), lambda i: (0, 0, i))
    flat = pl.BlockSpec((rows, lanes), lambda i: (0, i))
    return pl.pallas_call(
        hyena_kernel,
        grid=(channels // lanes,),
        out_shape=jax.ShapeDtypeStruct(query.shape, bf16),
        in_specs=[
            pl.BlockSpec(memory_space=pltpu.SMEM),
            block,
            block,
            block,
            pl.BlockSpec((rows, lanes), lambda i: (0, jnp.minimum(i, steps - 1))),
            pl.BlockSpec((rows, lanes), lambda i: (0, jnp.maximum(i - steps, 0))),
            pl.BlockSpec((rows, lanes), lambda i: (0, jnp.maximum(i - steps, 0))),
            flat,
            pl.BlockSpec((lanes // CH_GROUP, 2 * rows), lambda i: (i, 0)),
        ]
        + [pl.BlockSpec(memory_space=pl.ANY)] * len(after),
        out_specs=block,
        cost_estimate=TINY,
        name="hyena",
    )(place, query, key, value, *received, tail, wave, *after)


def attend_kernel(block_rows, q_ref, k_ref, v_ref, ck_ref, cv_ref, out_ref):
    sources, _, rows, width = k_ref.shape
    index = pl.program_id(1)
    scaling = 1.0 / math.sqrt(width)
    context = ck_ref.shape[1] * ck_ref.shape[3]
    contract = (((1,), (1,)), ((), ()))
    queries = q_ref[...].reshape(block_rows, width)
    per = block_rows // rows

    def fold(carried, scores, values):
        run_max, run_total, mixed = carried
        highest = jnp.maximum(run_max, jnp.max(scores, axis=1, keepdims=True))
        weights = jnp.exp((scores - highest) * scaling)
        shrink = jnp.exp((run_max - highest) * scaling)
        total = run_total * shrink + jnp.sum(weights, axis=1, keepdims=True)
        mixed = mixed * shrink + jnp.dot(weights.astype(bf16), values, preferred_element_type=f32)
        return highest, total, mixed

    def own(block):
        keys = k_ref[pl.ds(block * per, per), 0].reshape(block_rows, width)
        values = v_ref[pl.ds(block * per, per), 0].reshape(block_rows, width)
        return lax.dot_general(queries, keys, contract, preferred_element_type=f32), values

    scores, values = own(index)
    shape = (block_rows, block_rows)
    allowed = lax.broadcasted_iota(jnp.int32, shape, 1) <= lax.broadcasted_iota(jnp.int32, shape, 0)
    scores = jnp.where(allowed, scores, masked_score)
    start = (
        jnp.full((block_rows, 1), masked_score, f32),
        jnp.zeros((block_rows, 1), f32),
        jnp.zeros((block_rows, width), f32),
    )
    carried = fold(start, scores, values)
    carried = lax.fori_loop(0, index, lambda i, c: fold(c, *own(i)), carried)
    context_keys = ck_ref[0, :, 0].reshape(context, width)
    context_values = cv_ref[0, :, 0].reshape(context, width)
    scores = lax.dot_general(queries, context_keys, contract, preferred_element_type=f32)
    _, total, mixed = fold(carried, scores, context_values)
    out_ref[...] = (mixed / total).astype(bf16).reshape(out_ref.shape)


def attend(queries, keys, values, context):
    sources, heads, rows, width = queries.shape
    per = 2 if sources % 2 == 0 else 1
    whole = pl.BlockSpec((sources, 1, rows, width), lambda h, i: (0, h, 0, 0))
    part = pl.BlockSpec((per, 1, rows, width), lambda h, i: (i, h, 0, 0))

    def shared(which):
        return pl.BlockSpec((1, context.shape[1], 1) + context.shape[3:], lambda h, i: (h, 0, which, 0, 0))

    length, context_rows = sources * rows, context.shape[1] * context.shape[3]
    pairs = heads * length * (context_rows + (length + rows * per) // 2)
    return pl.pallas_call(
        functools.partial(attend_kernel, rows * per),
        grid=(heads, sources // per),
        out_shape=jax.ShapeDtypeStruct(queries.shape, bf16),
        in_specs=[part, whole, whole, shared(0), shared(1)],
        out_specs=part,
        cost_estimate=TINY,
        compiler_params=pltpu.CompilerParams(vmem_limit_bytes=VMEM),
        name="attend",
    )(queries, keys, values, context, context)


def attention_by_heads(cont_queries, cont_keys, cont_values, context_keys, context_values, left):
    peers = lax.axis_size("seq")
    rows, heads, width = cont_queries.shape
    share = heads // peers

    def by_owner(x):
        return x.reshape(x.shape[0], peers, share, width).transpose(1, 2, 0, 3)

    def exchange(x):
        return lax.all_to_all(x, "seq", split_axis=0, concat_axis=0, tiled=True)

    pair = exchange(jnp.stack([by_owner(context_keys), by_owner(context_values)], axis=2))
    context = pair.transpose(1, 0, 2, 3, 4)
    queries = exchange(by_owner(cont_queries))
    keys = exchange(by_owner(cont_keys))
    values = exchange(by_owner(cont_values))
    attended = exchange(attend(queries, keys, values, context))
    attention = attended.transpose(2, 0, 1, 3).reshape(rows, heads, width)
    keep = jnp.arange(rows)[:, None, None] < left
    return jnp.where(keep, attention, jnp.zeros((), bf16))


def pack_kernel(peers, side_ref, *refs):
    sources, outs, (heads_first, context_first) = refs[:5], refs[5:-2], refs[-2:]
    rows, heads, _ = sources[0].shape
    share = heads // peers
    each = share // WAVES
    for which, ref in enumerate(sources[:3]):
        heads_first[...] = jnp.transpose(ref[...], (1, 0, 2))
        for index, out in enumerate(outs):
            wave, partner = divmod(index, peers)
            start = (side_ref[2] ^ partner) * share + wave * each
            taken = heads_first[pl.ds(start, each)]
            for head in range(each):
                at = (which * each + head) * rows
                out[at : at + rows] = taken[head]
    for which, ref in enumerate(sources[3:]):
        context_first[...] = jnp.transpose(ref[...], (1, 0, 2))
        for partner, out in enumerate(outs[:peers]):
            start = (side_ref[2] ^ partner) * share + side_ref[1]
            at = 3 * each * rows + which * ref.shape[0]
            out[at : at + ref.shape[0]] = context_first[pl.ds(start, 1)][0]


def pack(arrays, side, peers):
    rows, heads, width = arrays[0].shape
    context_rows = arrays[3].shape[0]
    size = 3 * heads // peers // WAVES * rows
    sizes = [size + 2 * context_rows] * peers + [size] * (peers * (WAVES - 1))
    packed = pl.pallas_call(
        functools.partial(pack_kernel, peers),
        grid_spec=pltpu.PrefetchScalarGridSpec(
            num_scalar_prefetch=1,
            grid=(1,),
            in_specs=[pl.BlockSpec(x.shape, lambda i, s: (0, 0, 0)) for x in arrays],
            out_specs=[pl.BlockSpec((n, width), lambda i, s: (0, 0)) for n in sizes],
            scratch_shapes=[pltpu.VMEM((heads, rows, width), bf16), pltpu.VMEM((heads, context_rows, width), bf16)],
        ),
        out_shape=[jax.ShapeDtypeStruct((n, width), bf16) for n in sizes],
        cost_estimate=TINY,
        compiler_params=pltpu.CompilerParams(vmem_limit_bytes=VMEM),
        name="pack",
    )(side, *arrays)
    return [list(packed[wave * peers : (wave + 1) * peers]) for wave in range(WAVES)]


def gate_kernel(*refs):
    pass


def gate(x, after):
    anywhere = pl.BlockSpec(memory_space=pl.ANY)
    return pl.pallas_call(
        gate_kernel,
        in_specs=[anywhere] * (1 + len(after)),
        out_specs=anywhere,
        out_shape=jax.ShapeDtypeStruct(x.shape, x.dtype),
        input_output_aliases={0: 0},
        cost_estimate=TINY,
        name="gate",
    )(x, *after)


def gather_kernel(*refs):
    for index in range(refs[-1].shape[0]):
        refs[-1][index] = refs[index][...]


def gather(arrays, size, after):
    last = arrays[0].shape[0] // size - 1
    shape = (len(arrays), size, arrays[0].shape[1])
    return pl.pallas_call(
        gather_kernel,
        grid=(1,),
        in_specs=[pl.BlockSpec(shape[1:], lambda i: (last, 0))] * len(arrays)
        + [pl.BlockSpec(memory_space=pl.ANY)] * len(after),
        out_specs=pl.BlockSpec(shape, lambda i: (0, 0, 0)),
        out_shape=jax.ShapeDtypeStruct(shape, bf16),
        cost_estimate=TINY,
        name="gather",
    )(*arrays, *after)


def softmax_columns(pieces, scaling):
    highest = functools.reduce(jnp.maximum, [jnp.max(s, axis=0, keepdims=True) for s, _ in pieces])
    total = mixed = 0.0
    for scores, values in pieces:
        weights = jnp.exp((scores - highest) * scaling)
        total += jnp.sum(weights, axis=0, keepdims=True)
        mixed += lax.dot_general(values, weights.astype(bf16), (((0,), (0,)), ((), ())), preferred_element_type=f32)
    return mixed / total


def products(keys, queries):
    return lax.dot_general(keys, queries, (((1,), (1,)), ((), ())), preferred_element_type=f32)


def wave_kernel(wave, peers, side_ref, *refs):
    arrived, contexts, refs = refs[: 3 * peers], refs[3 * peers : 3 * peers + SIDE], refs[-peers - 6 :]
    outs, (qs, ks, vs, os, slots, sems) = refs[:peers], refs[peers:]
    rows, width = arrived[0].shape
    step = pl.program_id(0)
    each = slots.shape[0]
    scaling = 1.0 / math.sqrt(width)
    context_rows = slots.shape[2] // 2

    def each_copy(head, act):
        part = (wave * each + head) ^ side_ref[1]
        for number in range(SIDE):

            @pl.when(part == number)
            def _():
                act(pltpu.make_async_copy(contexts[number], slots.at[head], sems.at[head]))

    @pl.when(step == 0)
    def _():
        for head in range(each):
            each_copy(head, lambda copy: copy.start())

    places = [pl.ds(pl.multiple_of((side_ref[2] ^ partner) * rows, rows), rows) for partner in range(peers)]
    for partner, place in enumerate(places):
        qs[place] = arrived[3 * partner][...]
        ks[place] = arrived[3 * partner + 1][...]
        vs[place] = arrived[3 * partner + 2][...]

    for head in range(each):

        @pl.when(step == head)
        def _():
            each_copy(head, lambda copy: copy.wait())

    context_keys = slots[step, :, :context_rows].reshape(peers * context_rows, width)
    context_values = slots[step, :, context_rows:].reshape(peers * context_rows, width)
    block = min(BLOCK, peers * rows)
    for index in range(peers * rows // block):
        here = slice(index * block, (index + 1) * block)
        queries = qs[here]
        pieces = [(products(context_keys, queries), context_values)]
        if index > 0:
            before = slice(0, index * block)
            pieces.append((products(ks[before], queries), vs[before]))
        scores = products(ks[here], queries)
        allowed = lax.broadcasted_iota(jnp.int32, scores.shape, 0) <= lax.broadcasted_iota(
            jnp.int32, scores.shape, 1
        )
        pieces.append((jnp.where(allowed, scores, masked_score), vs[here]))
        os[here] = softmax_columns(pieces, scaling).T.astype(bf16)
    for partner, place in enumerate(places):
        outs[partner][0] = os[place]


def attend_wave(wave, arrived, contexts, side, after):
    peers = len(arrived)
    rows, width = LANES, arrived[0].shape[1]
    each = arrived[0].shape[0] // rows // 3

    def taken(which):
        return pl.BlockSpec((rows, width), lambda i, s: (which * each + i, 0))

    result = pl.BlockSpec((1, rows, width), lambda i, s: (i, 0, 0))
    return pl.pallas_call(
        functools.partial(wave_kernel, wave, peers),
        grid_spec=pltpu.PrefetchScalarGridSpec(
            num_scalar_prefetch=1,
            grid=(each,),
            in_specs=[taken(which) for _ in arrived for which in range(3)]
            + [pl.BlockSpec(memory_space=pl.ANY)] * (SIDE + len(after)),
            out_specs=[result] * peers,
            scratch_shapes=[pltpu.VMEM((peers * rows, width), bf16)] * 4
            + [pltpu.VMEM((each,) + contexts[0].shape, bf16), pltpu.SemaphoreType.DMA((each,))],
        ),
        out_shape=[jax.ShapeDtypeStruct((each, rows, width), bf16)] * peers,
        cost_estimate=TINY,
        compiler_params=pltpu.CompilerParams(vmem_limit_bytes=VMEM),
        name="attend_wave",
    )(side, *[x for x in arrived for _ in range(3)], *contexts, *after)


def unpack_kernel(peers, side_ref, *refs):
    arrived, (out, heads_first) = refs[:-2], refs[-2:]
    each = arrived[0].shape[0]
    for index, ref in enumerate(arrived):
        wave, partner = divmod(index, peers)
        heads_first[pl.ds((side_ref[2] ^ partner) * each * WAVES + wave * each, each)] = ref[...]
    result = jnp.transpose(heads_first[...], (1, 0, 2)).astype(f32)
    place = lax.broadcasted_iota(jnp.int32, result.shape, 0) + pl.program_id(0) * result.shape[0]
    out[...] = jnp.where(place < side_ref[0], result, 0.0).astype(bf16)


def unpack(arrived, side):
    each, rows, width = arrived[0].shape
    heads = each * len(arrived)
    step = rows // 2
    return pl.pallas_call(
        functools.partial(unpack_kernel, len(arrived) // WAVES),
        grid_spec=pltpu.PrefetchScalarGridSpec(
            num_scalar_prefetch=1,
            grid=(rows // step,),
            in_specs=[pl.BlockSpec((each, step, width), lambda i, s: (0, i, 0))] * len(arrived),
            out_specs=pl.BlockSpec((step, heads, width), lambda i, s: (i, 0, 0)),
            scratch_shapes=[pltpu.VMEM((heads, step, width), bf16)],
        ),
        out_shape=jax.ShapeDtypeStruct((rows, heads, width), bf16),
        cost_estimate=TINY,
        compiler_params=pltpu.CompilerParams(vmem_limit_bytes=VMEM),
        name="unpack",
    )(side, *arrived)


def in_waves(arrays, left, key, value, constants, finish):
    peers = lax.axis_size("seq")
    cands = lax.axis_size("cand")
    side = jnp.stack([left, lax.axis_index("cand"), lax.axis_index("seq")]).astype(jnp.int32)

    def exchange(parts, chosen):
        parts = list(parts)
        for k in chosen:
            parts[k] = lax.ppermute(parts[k], "seq", [(i, i ^ k) for i in range(peers)])
        return parts

    def swap(x, k):
        return lax.ppermute(x, "cand", [(i, i ^ k) for i in range(cands)])

    everyone, near_by, across_half = range(1, peers), range(1, peers // 2), range(peers // 2, peers)
    one, two = pack(arrays, side, peers)
    one = exchange(one, everyone)
    two = exchange(two, across_half)
    received = brought((key.astype(f32) * value.astype(f32)).astype(bf16))
    context = gather(one, 2 * arrays[3].shape[0], constants)
    across = swap(context, 2)
    contexts = [context, swap(context, 1), across, swap(across, 1)]

    first = attend_wave(0, one, contexts, side, tuple(two[k] for k in across_half[:EARLY]))
    two = [gate(x, (first[0],)) if k in near_by else x for k, x in enumerate(two)]
    two = exchange(two, near_by)
    hyena_out = finish(received, (first[0],))
    second = attend_wave(1, two, contexts, side, (hyena_out,))
    return unpack(exchange(first, everyone) + exchange(second, everyone), side), hyena_out


def brought(product):
    peers = lax.axis_size("seq")
    half = product.shape[1] // 2
    near, far = product[:, :half], product[:, half:]
    near = lax.ppermute(near, "seq", [(i, i + 1) for i in range(peers - 1)])
    odd = lax.ppermute(far, "seq", [(i, i ^ 1) for i in range(peers)])
    even = lax.ppermute(odd, "seq", [(i, i + 2) for i in range(0, peers - 2, 2)])
    return near, even, odd


def local(
    hyena_query,
    hyena_key,
    hyena_value,
    hyena_filters,
    context_tail,
    cont_queries,
    cont_keys,
    cont_values,
    context_keys,
    context_values,
    lengths,
):
    peers = lax.axis_size("seq")
    me = lax.axis_index("seq")
    rows = hyena_key.shape[1]
    heads = cont_queries.shape[2]
    left = (lengths[0] - me * rows).astype(jnp.int32)

    place = jnp.stack([me.astype(jnp.int32), left])

    wave = jnp.pad(hyena_filters[::-1], ((1, 2 * rows - hyena_filters.shape[0] - 1), (0, 0))).T
    constants = (wave, jnp.pad(context_tail, ((1, 0), (0, 0))))

    def finish(received, after):
        return hyena(hyena_query, hyena_key, hyena_value, received, constants, place, after)

    share = heads // peers
    waves = share == SIDE and lax.axis_size("cand") == SIDE and peers & (peers - 1) == 0
    arrays = (cont_queries[0], cont_keys[0], cont_values[0], context_keys, context_values)
    key, value = hyena_key[0], hyena_value[0]
    if waves:
        attention_out, hyena_out = in_waves(arrays, left, key, value, constants, finish)
    else:
        attention_out = attention_by_heads(*arrays, left)
        hyena_out = finish(brought((key.astype(f32) * value.astype(f32)).astype(bf16)), ())
    return (hyena_out, attention_out[None])


def solution(mesh):
    placed = (
        P("cand", "seq", None),
        P("cand", "seq", None),
        P("cand", "seq", None),
        P(),
        P(),
        P("cand", "seq", None, None),
        P("cand", "seq", None, None),
        P("cand", "seq", None, None),
        P("seq", None, None),
        P("seq", None, None),
        P("cand"),
    )
    return jax.shard_map(
        local,
        mesh=mesh,
        in_specs=placed,
        out_specs=(P("cand", "seq", None), P("cand", "seq", None, None)),
        check_vma=False,
    )
```

```python
import functools
import math

import jax
import jax.numpy as jnp
from jax import lax
from jax.experimental import pallas as pl
from jax.experimental.pallas import tpu as pltpu
from jax.sharding import PartitionSpec as P

CH_GROUP = 16
LANES = 128
VMEM = 56 * 1024 * 1024
WAVES = 2
SIDE = 4
BLOCK = 512
EARLY = 2

masked_score = -1e30
TINY = pl.CostEstimate(flops=1, bytes_accessed=1, transcendentals=0)

bf16 = jnp.bfloat16
f32 = jnp.float32


def hyena_kernel(place_ref, query_ref, key_ref, value_ref, near_ref, even_ref, odd_ref, tail_ref, wave_ref, *refs):
    rows, lanes = key_ref.shape[1], key_ref.shape[2]
    out_ref = refs[-1]
    groups = LANES // CH_GROUP
    product = (key_ref[0].astype(f32) * value_ref[0].astype(f32)).astype(bf16)
    shape = (rows, lanes)
    first = jnp.broadcast_to(place_ref[0], shape) == 0
    even = jnp.broadcast_to(place_ref[0] % 2, shape) == 0
    lower = jnp.broadcast_to(pl.program_id(0), shape) < pl.num_programs(0) // 2
    earlier = jnp.where(even, even_ref[...].astype(f32), odd_ref[...].astype(f32))
    earlier = jnp.where(lower, near_ref[...].astype(f32), earlier)
    earlier = jnp.where(first, tail_ref[...].astype(f32), earlier)
    extended = jnp.concatenate([earlier.astype(bf16), product], axis=0)
    channel = lax.broadcasted_iota(jnp.int32, (rows, LANES), 1) // CH_GROUP
    tiles = []
    for tile in range(lanes // LANES):
        columns = extended[:, tile * LANES : (tile + 1) * LANES]
        twice = jnp.concatenate([columns, columns], axis=0)
        convolved = jnp.zeros((rows, LANES), f32)
        for group in range(groups):
            line = tile * groups + group
            wave = jnp.broadcast_to(wave_ref[line : line + 1, :], (rows, 2 * rows))
            taps = pltpu.roll(wave, 0, 1, stride=1, stride_axis=0)
            high = taps.astype(bf16)
            low = (taps - high.astype(f32)).astype(bf16)
            term = jnp.dot(jnp.concatenate([high, low], axis=1), twice, preferred_element_type=f32)
            convolved = jnp.where(channel == group, term, convolved)
        tiles.append(convolved)
    convolved = jnp.concatenate(tiles, axis=1)
    places = lax.broadcasted_iota(jnp.int32, (rows, lanes), 0)
    gated = query_ref[0].astype(f32) * convolved
    out_ref[0] = jnp.where(places < place_ref[1], gated, 0.0).astype(bf16)


def hyena(query, key, value, received, constants, place, after):
    _, rows, channels = key.shape
    wave, tail = constants
    groups = LANES // CH_GROUP
    lanes = math.gcd(channels // 2, 8 * LANES)
    steps = channels // lanes // 2
    block = pl.BlockSpec((1, rows, lanes), lambda i: (0, 0, i))
    flat = pl.BlockSpec((rows, lanes), lambda i: (0, i))
    return pl.pallas_call(
        hyena_kernel,
        grid=(channels // lanes,),
        out_shape=jax.ShapeDtypeStruct(query.shape, bf16),
        in_specs=[
            pl.BlockSpec(memory_space=pltpu.SMEM),
            block,
            block,
            block,
            pl.BlockSpec((rows, lanes), lambda i: (0, jnp.minimum(i, steps - 1))),
            pl.BlockSpec((rows, lanes), lambda i: (0, jnp.maximum(i - steps, 0))),
            pl.BlockSpec((rows, lanes), lambda i: (0, jnp.maximum(i - steps, 0))),
            flat,
            pl.BlockSpec((lanes // CH_GROUP, 2 * rows), lambda i: (i, 0)),
        ]
        + [pl.BlockSpec(memory_space=pl.ANY)] * len(after),
        out_specs=block,
        cost_estimate=TINY,
        name="hyena",
    )(place, query, key, value, *received, tail, wave, *after)


def attend_kernel(block_rows, q_ref, k_ref, v_ref, ck_ref, cv_ref, out_ref):
    sources, _, rows, width = k_ref.shape
    index = pl.program_id(1)
    scaling = 1.0 / math.sqrt(width)
    context = ck_ref.shape[1] * ck_ref.shape[3]
    contract = (((1,), (1,)), ((), ()))
    queries = q_ref[...].reshape(block_rows, width)
    per = block_rows // rows

    def fold(carried, scores, values):
        run_max, run_total, mixed = carried
        highest = jnp.maximum(run_max, jnp.max(scores, axis=1, keepdims=True))
        weights = jnp.exp((scores - highest) * scaling)
        shrink = jnp.exp((run_max - highest) * scaling)
        total = run_total * shrink + jnp.sum(weights, axis=1, keepdims=True)
        mixed = mixed * shrink + jnp.dot(weights.astype(bf16), values, preferred_element_type=f32)
        return highest, total, mixed

    def own(block):
        keys = k_ref[pl.ds(block * per, per), 0].reshape(block_rows, width)
        values = v_ref[pl.ds(block * per, per), 0].reshape(block_rows, width)
        return lax.dot_general(queries, keys, contract, preferred_element_type=f32), values

    scores, values = own(index)
    shape = (block_rows, block_rows)
    allowed = lax.broadcasted_iota(jnp.int32, shape, 1) <= lax.broadcasted_iota(jnp.int32, shape, 0)
    scores = jnp.where(allowed, scores, masked_score)
    start = (
        jnp.full((block_rows, 1), masked_score, f32),
        jnp.zeros((block_rows, 1), f32),
        jnp.zeros((block_rows, width), f32),
    )
    carried = fold(start, scores, values)
    carried = lax.fori_loop(0, index, lambda i, c: fold(c, *own(i)), carried)
    context_keys = ck_ref[0, :, 0].reshape(context, width)
    context_values = cv_ref[0, :, 0].reshape(context, width)
    scores = lax.dot_general(queries, context_keys, contract, preferred_element_type=f32)
    _, total, mixed = fold(carried, scores, context_values)
    out_ref[...] = (mixed / total).astype(bf16).reshape(out_ref.shape)


def attend(queries, keys, values, context):
    sources, heads, rows, width = queries.shape
    per = 2 if sources % 2 == 0 else 1
    whole = pl.BlockSpec((sources, 1, rows, width), lambda h, i: (0, h, 0, 0))
    part = pl.BlockSpec((per, 1, rows, width), lambda h, i: (i, h, 0, 0))

    def shared(which):
        return pl.BlockSpec((1, context.shape[1], 1) + context.shape[3:], lambda h, i: (h, 0, which, 0, 0))

    length, context_rows = sources * rows, context.shape[1] * context.shape[3]
    pairs = heads * length * (context_rows + (length + rows * per) // 2)
    return pl.pallas_call(
        functools.partial(attend_kernel, rows * per),
        grid=(heads, sources // per),
        out_shape=jax.ShapeDtypeStruct(queries.shape, bf16),
        in_specs=[part, whole, whole, shared(0), shared(1)],
        out_specs=part,
        cost_estimate=TINY,
        compiler_params=pltpu.CompilerParams(vmem_limit_bytes=VMEM),
        name="attend",
    )(queries, keys, values, context, context)


def attention_by_heads(cont_queries, cont_keys, cont_values, context_keys, context_values, left):
    peers = lax.axis_size("seq")
    rows, heads, width = cont_queries.shape
    share = heads // peers

    def by_owner(x):
        return x.reshape(x.shape[0], peers, share, width).transpose(1, 2, 0, 3)

    def exchange(x):
        return lax.all_to_all(x, "seq", split_axis=0, concat_axis=0, tiled=True)

    pair = exchange(jnp.stack([by_owner(context_keys), by_owner(context_values)], axis=2))
    context = pair.transpose(1, 0, 2, 3, 4)
    queries = exchange(by_owner(cont_queries))
    keys = exchange(by_owner(cont_keys))
    values = exchange(by_owner(cont_values))
    attended = exchange(attend(queries, keys, values, context))
    attention = attended.transpose(2, 0, 1, 3).reshape(rows, heads, width)
    keep = jnp.arange(rows)[:, None, None] < left
    return jnp.where(keep, attention, jnp.zeros((), bf16))


def pack_kernel(peers, side_ref, *refs):
    sources, outs, (heads_first, context_first) = refs[:5], refs[5:-2], refs[-2:]
    rows, heads, _ = sources[0].shape
    share = heads // peers
    each = share // WAVES
    for which, ref in enumerate(sources[:3]):
        heads_first[...] = jnp.transpose(ref[...], (1, 0, 2))
        for index, out in enumerate(outs):
            wave, partner = divmod(index, peers)
            start = (side_ref[2] ^ partner) * share + wave * each
            taken = heads_first[pl.ds(start, each)]
            for head in range(each):
                at = (which * each + head) * rows
                out[at : at + rows] = taken[head]
    for which, ref in enumerate(sources[3:]):
        context_first[...] = jnp.transpose(ref[...], (1, 0, 2))
        for partner, out in enumerate(outs[:peers]):
            start = (side_ref[2] ^ partner) * share + side_ref[1]
            at = 3 * each * rows + which * ref.shape[0]
            out[at : at + ref.shape[0]] = context_first[pl.ds(start, 1)][0]


def pack(arrays, side, peers):
    rows, heads, width = arrays[0].shape
    context_rows = arrays[3].shape[0]
    size = 3 * heads // peers // WAVES * rows
    sizes = [size + 2 * context_rows] * peers + [size] * (peers * (WAVES - 1))
    packed = pl.pallas_call(
        functools.partial(pack_kernel, peers),
        grid_spec=pltpu.PrefetchScalarGridSpec(
            num_scalar_prefetch=1,
            grid=(1,),
            in_specs=[pl.BlockSpec(x.shape, lambda i, s: (0, 0, 0)) for x in arrays],
            out_specs=[pl.BlockSpec((n, width), lambda i, s: (0, 0)) for n in sizes],
            scratch_shapes=[pltpu.VMEM((heads, rows, width), bf16), pltpu.VMEM((heads, context_rows, width), bf16)],
        ),
        out_shape=[jax.ShapeDtypeStruct((n, width), bf16) for n in sizes],
        cost_estimate=TINY,
        compiler_params=pltpu.CompilerParams(vmem_limit_bytes=VMEM),
        name="pack",
    )(side, *arrays)
    return [list(packed[wave * peers : (wave + 1) * peers]) for wave in range(WAVES)]


def gate_kernel(*refs):
    pass


def gate(x, after):
    anywhere = pl.BlockSpec(memory_space=pl.ANY)
    return pl.pallas_call(
        gate_kernel,
        in_specs=[anywhere] * (1 + len(after)),
        out_specs=anywhere,
        out_shape=jax.ShapeDtypeStruct(x.shape, x.dtype),
        input_output_aliases={0: 0},
        cost_estimate=TINY,
        name="gate",
    )(x, *after)


def gather_kernel(*refs):
    for index in range(refs[-1].shape[0]):
        refs[-1][index] = refs[index][...]


def gather(arrays, size, after):
    last = arrays[0].shape[0] // size - 1
    shape = (len(arrays), size, arrays[0].shape[1])
    return pl.pallas_call(
        gather_kernel,
        grid=(1,),
        in_specs=[pl.BlockSpec(shape[1:], lambda i: (last, 0))] * len(arrays)
        + [pl.BlockSpec(memory_space=pl.ANY)] * len(after),
        out_specs=pl.BlockSpec(shape, lambda i: (0, 0, 0)),
        out_shape=jax.ShapeDtypeStruct(shape, bf16),
        cost_estimate=TINY,
        name="gather",
    )(*arrays, *after)


def softmax_columns(pieces, scaling):
    highest = functools.reduce(jnp.maximum, [jnp.max(s, axis=0, keepdims=True) for s, _ in pieces])
    total = mixed = 0.0
    for scores, values in pieces:
        weights = jnp.exp((scores - highest) * scaling)
        total += jnp.sum(weights, axis=0, keepdims=True)
        mixed += lax.dot_general(values, weights.astype(bf16), (((0,), (0,)), ((), ())), preferred_element_type=f32)
    return mixed / total


def products(keys, queries):
    return lax.dot_general(keys, queries, (((1,), (1,)), ((), ())), preferred_element_type=f32)


def wave_kernel(wave, peers, side_ref, *refs):
    arrived, contexts, refs = refs[: 3 * peers], refs[3 * peers : 3 * peers + SIDE], refs[-peers - 6 :]
    outs, (qs, ks, vs, os, slots, sems) = refs[:peers], refs[peers:]
    rows, width = arrived[0].shape
    step = pl.program_id(0)
    each = slots.shape[0]
    scaling = 1.0 / math.sqrt(width)
    context_rows = slots.shape[2] // 2

    def each_copy(head, act):
        part = (wave * each + head) ^ side_ref[1]
        for number in range(SIDE):

            @pl.when(part == number)
            def _():
                act(pltpu.make_async_copy(contexts[number], slots.at[head], sems.at[head]))

    @pl.when(step == 0)
    def _():
        for head in range(each):
            each_copy(head, lambda copy: copy.start())

    places = [pl.ds(pl.multiple_of((side_ref[2] ^ partner) * rows, rows), rows) for partner in range(peers)]
    for partner, place in enumerate(places):
        qs[place] = arrived[3 * partner][...]
        ks[place] = arrived[3 * partner + 1][...]
        vs[place] = arrived[3 * partner + 2][...]

    for head in range(each):

        @pl.when(step == head)
        def _():
            each_copy(head, lambda copy: copy.wait())

    context_keys = slots[step, :, :context_rows].reshape(peers * context_rows, width)
    context_values = slots[step, :, context_rows:].reshape(peers * context_rows, width)
    block = min(BLOCK, peers * rows)
    for index in range(peers * rows // block):
        here = slice(index * block, (index + 1) * block)
        queries = qs[here]
        pieces = [(products(context_keys, queries), context_values)]
        if index > 0:
            before = slice(0, index * block)
            pieces.append((products(ks[before], queries), vs[before]))
        scores = products(ks[here], queries)
        allowed = lax.broadcasted_iota(jnp.int32, scores.shape, 0) <= lax.broadcasted_iota(
            jnp.int32, scores.shape, 1
        )
        pieces.append((jnp.where(allowed, scores, masked_score), vs[here]))
        os[here] = softmax_columns(pieces, scaling).T.astype(bf16)
    for partner, place in enumerate(places):
        outs[partner][0] = os[place]


def attend_wave(wave, arrived, contexts, side, after):
    peers = len(arrived)
    rows, width = LANES, arrived[0].shape[1]
    each = arrived[0].shape[0] // rows // 3

    def taken(which):
        return pl.BlockSpec((rows, width), lambda i, s: (which * each + i, 0))

    result = pl.BlockSpec((1, rows, width), lambda i, s: (i, 0, 0))
    return pl.pallas_call(
        functools.partial(wave_kernel, wave, peers),
        grid_spec=pltpu.PrefetchScalarGridSpec(
            num_scalar_prefetch=1,
            grid=(each,),
            in_specs=[taken(which) for _ in arrived for which in range(3)]
            + [pl.BlockSpec(memory_space=pl.ANY)] * (SIDE + len(after)),
            out_specs=[result] * peers,
            scratch_shapes=[pltpu.VMEM((peers * rows, width), bf16)] * 4
            + [pltpu.VMEM((each,) + contexts[0].shape, bf16), pltpu.SemaphoreType.DMA((each,))],
        ),
        out_shape=[jax.ShapeDtypeStruct((each, rows, width), bf16)] * peers,
        cost_estimate=TINY,
        compiler_params=pltpu.CompilerParams(vmem_limit_bytes=VMEM),
        name="attend_wave",
    )(side, *[x for x in arrived for _ in range(3)], *contexts, *after)


def unpack_kernel(peers, side_ref, *refs):
    arrived, (out, heads_first) = refs[:-2], refs[-2:]
    each = arrived[0].shape[0]
    for index, ref in enumerate(arrived):
        wave, partner = divmod(index, peers)
        heads_first[pl.ds((side_ref[2] ^ partner) * each * WAVES + wave * each, each)] = ref[...]
    result = jnp.transpose(heads_first[...], (1, 0, 2)).astype(f32)
    place = lax.broadcasted_iota(jnp.int32, result.shape, 0) + pl.program_id(0) * result.shape[0]
    out[...] = jnp.where(place < side_ref[0], result, 0.0).astype(bf16)


def unpack(arrived, side):
    each, rows, width = arrived[0].shape
    heads = each * len(arrived)
    step = rows // 2
    return pl.pallas_call(
        functools.partial(unpack_kernel, len(arrived) // WAVES),
        grid_spec=pltpu.PrefetchScalarGridSpec(
            num_scalar_prefetch=1,
            grid=(rows // step,),
            in_specs=[pl.BlockSpec((each, step, width), lambda i, s: (0, i, 0))] * len(arrived),
            out_specs=pl.BlockSpec((step, heads, width), lambda i, s: (i, 0, 0)),
            scratch_shapes=[pltpu.VMEM((heads, step, width), bf16)],
        ),
        out_shape=jax.ShapeDtypeStruct((rows, heads, width), bf16),
        cost_estimate=TINY,
        compiler_params=pltpu.CompilerParams(vmem_limit_bytes=VMEM),
        name="unpack",
    )(side, *arrived)


def in_waves(arrays, left, key, value, constants, finish):
    peers = lax.axis_size("seq")
    cands = lax.axis_size("cand")
    side = jnp.stack([left, lax.axis_index("cand"), lax.axis_index("seq")]).astype(jnp.int32)

    def exchange(parts, chosen):
        parts = list(parts)
        for k in chosen:
            parts[k] = lax.ppermute(parts[k], "seq", [(i, i ^ k) for i in range(peers)])
        return parts

    def swap(x, k):
        return lax.ppermute(x, "cand", [(i, i ^ k) for i in range(cands)])

    everyone, near_by, across_half = range(1, peers), range(1, peers // 2), range(peers // 2, peers)
    one, two = pack(arrays, side, peers)
    one = exchange(one, everyone)
    two = exchange(two, across_half)
    received = brought((key.astype(f32) * value.astype(f32)).astype(bf16))
    context = gather(one, 2 * arrays[3].shape[0], constants)
    across = swap(context, 2)
    contexts = [context, swap(context, 1), across, swap(across, 1)]

    first = attend_wave(0, one, contexts, side, tuple(two[k] for k in across_half[:EARLY]))
    two = [gate(x, (first[0],)) if k in near_by else x for k, x in enumerate(two)]
    two = exchange(two, near_by)
    hyena_out = finish(received, (first[0],))
    second = attend_wave(1, two, contexts, side, (hyena_out,))
    return unpack(exchange(first, everyone) + exchange(second, everyone), side), hyena_out


def brought(product):
    peers = lax.axis_size("seq")
    half = product.shape[1] // 2
    near, far = product[:, :half], product[:, half:]
    near = lax.ppermute(near, "seq", [(i, i + 1) for i in range(peers - 1)])
    odd = lax.ppermute(far, "seq", [(i, i ^ 1) for i in range(peers)])
    even = lax.ppermute(odd, "seq", [(i, i + 2) for i in range(0, peers - 2, 2)])
    return near, even, odd


def local(
    hyena_query,
    hyena_key,
    hyena_value,
    hyena_filters,
    context_tail,
    cont_queries,
    cont_keys,
    cont_values,
    context_keys,
    context_values,
    lengths,
):
    peers = lax.axis_size("seq")
    me = lax.axis_index("seq")
    rows = hyena_key.shape[1]
    heads = cont_queries.shape[2]
    left = (lengths[0] - me * rows).astype(jnp.int32)

    place = jnp.stack([me.astype(jnp.int32), left])

    wave = jnp.pad(hyena_filters[::-1], ((1, 2 * rows - hyena_filters.shape[0] - 1), (0, 0))).T
    constants = (wave, jnp.pad(context_tail, ((1, 0), (0, 0))))

    def finish(received, after):
        return hyena(hyena_query, hyena_key, hyena_value, received, constants, place, after)

    share = heads // peers
    waves = share == SIDE and lax.axis_size("cand") == SIDE and peers & (peers - 1) == 0
    arrays = (cont_queries[0], cont_keys[0], cont_values[0], context_keys, context_values)
    key, value = hyena_key[0], hyena_value[0]
    if waves:
        attention_out, hyena_out = in_waves(arrays, left, key, value, constants, finish)
    else:
        attention_out = attention_by_heads(*arrays, left)
        hyena_out = finish(brought((key.astype(f32) * value.astype(f32)).astype(bf16)), ())
    return (hyena_out, attention_out[None])


def solution(mesh):
    placed = (
        P("cand", "seq", None),
        P("cand", "seq", None),
        P("cand", "seq", None),
        P(),
        P(),
        P("cand", "seq", None, None),
        P("cand", "seq", None, None),
        P("cand", "seq", None, None),
        P("seq", None, None),
        P("seq", None, None),
        P("cand"),
    )
    return jax.shard_map(
        local,
        mesh=mesh,
        in_specs=placed,
        out_specs=(P("cand", "seq", None), P("cand", "seq", None, None)),
        check_vma=False,
    )
```
